128 devices in a mesh: head: 8 (over y, core), qblk: 16 (over z, x).
Axes of the slice: x: 4, y: 4, z: 4, core: 2. Of those that a mesh axis runs over, the one named last changes fastest.
Arguments:
- q_absorbed: bfloat16 [4096, 128, 576], P('qblk', 'head'), may hold values from -64 to 64
- key_cache: bfloat16 [512, 704, 128], P('qblk'), may hold values from -8 to 8
- index_input: bfloat16 [4096, 1536], P('qblk'), may hold values from -6 to 6
- index_weight: bfloat16 [1536, 8192], P(None, 'head'), may hold values from -0.15625 to 0.15625
- head_weights: float32 [4096, 64], P('qblk', 'head'), may hold values from -0.24 to 0.24
- block_ids: int32 [32, 16], replicated, may hold values from 0 to 511, as said below
- block_counts: int32 [32], replicated, may hold values from 1 to 16, as said below
Outputs:
- weight_grad: float32 [1536, 8192], P(None, 'head')
- cross_entropy: float32 [4096], P(('qblk', 'head'))
The draws below stay inside these ranges and needn't reach their ends.
Inputs may be any that keep to these rules, and one draw needn't show every extreme that they name: `block_ids`: row g holds 16 distinct block numbers; entry 0 is 480 + g and all others are smaller. Of one row's entries at most 3 lie in one run of 32 block numbers starting at a multiple of 32, and in every row some such run holds exactly 3. `block_counts`: in every draw, for some index of qblk all 2 of its query blocks use all 16 slots.
All inputs are finite; a program needn't handle non-finite values.
Results may differ from the reference program's by a relative error of at most 0.03.
The reference program's roundings to bfloat16 on the way (of `index_query`, `affinity_grad` and `query_grad`) count: a program that leaves them out, or rounds other values in their place, can miss the bound.
Values may be sent and summed in bfloat16 or wider, within the bound.
No kernel may reach another device: no remote copies, remote signals or barrier semaphores. Data moves between devices by JAX's collectives and lax.ppermute only.
A program may use at most 128 MiB of HBM per device.

```python
import jax
import jax.numpy as jnp
from jax import lax

H = 128
DL = 512
DR = 64
IH = 64
ID = 128
DQ = 1536
BLK = 128
SEL = 16
CAP1 = 3
QBLK_DEV = 2
KBLK_DEV = 32
QBLKS = 32
KBLKS = 512
QUERIES = 4096


def cache_values(key):
    shape = (KBLKS, DL + DR + ID, BLK)
    normal = jnp.clip(jax.random.normal(key, shape, jnp.float32), -4.0, 4.0)
    return normal


def draw_key_cache(key, part):
    values = cache_values(key)
    return values.astype(jnp.bfloat16)


def draw_q_absorbed(key, part):
    key = jax.random.fold_in(key, 23)
    queries = jnp.clip(jax.random.normal(key, (QUERIES, H, DL + DR), jnp.float32), -4.0, 4.0)
    return queries.astype(jnp.bfloat16)


def draw_block_ids(key, part):
    key = jax.random.fold_in(key, 31)
    hot_shard = jax.random.randint(jax.random.fold_in(key, 1), (), 0, (KBLKS - QBLKS) // KBLK_DEV)
    rough_scores = jax.random.randint(jax.random.fold_in(key, 2), (QBLKS, KBLKS), 0, 4096)
    column = jnp.arange(KBLKS, dtype=jnp.int32)[None, :]
    diagonal = (KBLKS - QBLKS + jnp.arange(QBLKS, dtype=jnp.int32))[:, None]
    score_unit = 4096 * KBLKS
    scores = rough_scores * KBLKS + column
    scores = scores + jnp.where((column // KBLK_DEV == hot_shard) & (column % KBLK_DEV < 4), score_unit, 0)
    scores = scores + jnp.where(column == diagonal, 2 * score_unit, 0)
    allowed = column <= diagonal
    scores = jnp.where(allowed, scores, -1 - column)
    grouped = scores.reshape(QBLKS, KBLKS // KBLK_DEV, KBLK_DEV)
    ranking = jnp.sum((grouped[:, :, None, :] > grouped[:, :, :, None]).astype(jnp.int32), axis=3)
    keep_mask = allowed & (ranking.reshape(QBLKS, KBLKS) < CAP1)
    final_scores = jnp.where(keep_mask, scores, -1 - column)
    _, picked = lax.top_k(final_scores, SEL)
    return picked.astype(jnp.int32)


def draw_block_counts(key, part):
    key = jax.random.fold_in(key, 41)
    counts = jax.random.randint(jax.random.fold_in(key, 1), (QBLKS,), 1, SEL + 1)
    full_group = jax.random.randint(jax.random.fold_in(key, 2), (), 0, QBLKS // QBLK_DEV)
    groups = jnp.arange(QBLKS, dtype=jnp.int32) // QBLK_DEV
    return jnp.where(groups == full_group, SEL, counts).astype(jnp.int32)


def block_scale(stream_key, extent, split, low, high):
    factor_of = 1.0
    for dim, parts in split:
        heights = jax.random.uniform(jax.random.fold_in(jax.random.fold_in(stream_key, 6), dim), (parts,), jnp.float32, low / len(split), high / len(split))
        factor_of = factor_of * jnp.repeat(jnp.exp(heights), extent[dim] // parts).reshape((-1,) + (1,) * (len(extent) - 1 - dim))
    return factor_of


def bell_draw(own_key, extent, deviation, limit, cuts=(), held_as=jnp.bfloat16):
    entries = deviation * jax.random.normal(own_key, extent, jnp.float32)
    if cuts:
        entries = entries * block_scale(own_key, extent, cuts, -0.22, 0.18)
    return jnp.clip(entries, -limit, limit).astype(held_as)


def setup_inputs(seed: int = 0) -> dict:
    keys = jax.random.split(jax.random.key(seed), 8)
    return {
        "q_absorbed": draw_q_absorbed(jax.random.fold_in(keys[7], 71), 0),
        "key_cache": draw_key_cache(jax.random.fold_in(keys[7], 71), 0),
        "index_input": bell_draw(keys[2], (QUERIES, DQ), 1.0, 6.0, ((0, 16),)),
        "index_weight": bell_draw(keys[3], (DQ, IH * ID), DQ ** -0.5, 0.15625, ((1, 8),)),
        "head_weights": bell_draw(keys[4], (QUERIES, IH), 0.04, 0.24, ((0, 16), (1, 8)), jnp.float32),
        "block_ids": draw_block_ids(jax.random.fold_in(keys[7], 71), 0),
        "block_counts": draw_block_counts(jax.random.fold_in(keys[7], 71), 0),
    }


score_scale = 192.0 ** -0.5
masked_value = -1e30


def reference(q_absorbed, key_cache, index_input, index_weight, head_weights, block_ids, block_counts):
    query_rows = jnp.arange(BLK, dtype=jnp.int32)
    slot_iota = jnp.arange(SEL, dtype=jnp.int32)
    total_queries = QBLKS * BLK

    def per_block(block_index):
        start = (block_index * BLK).astype(jnp.int32)
        query_tile = lax.dynamic_slice_in_dim(q_absorbed, start, BLK, 0).astype(jnp.float32)
        picked = jnp.take(key_cache, block_ids[block_index], axis=0)
        latent = picked[:, :DL + DR, :].astype(jnp.float32)
        index_keys = picked[:, DL + DR:, :].astype(jnp.float32)
        valid = (slot_iota[None, :, None] < block_counts[block_index]) & (
            (slot_iota[None, :, None] > 0) | (query_rows[None, None, :] <= query_rows[:, None, None]))
        scores = jnp.einsum('qhd,sdk->qhsk', query_tile, latent) * score_scale
        scores = jnp.where(valid[:, None], scores, masked_value)
        row_peak = jnp.max(scores, axis=(2, 3), keepdims=True)
        weights_exp = jnp.exp(scores - row_peak)
        attention = weights_exp / jnp.sum(weights_exp, axis=(2, 3), keepdims=True)
        target = jnp.sum(attention, axis=1) / H
        input_rows = lax.dynamic_slice_in_dim(index_input, start, BLK, 0)
        index_query = jnp.dot(input_rows, index_weight, preferred_element_type=jnp.float32).astype(jnp.bfloat16)
        index_query = index_query.reshape(BLK, IH, ID).astype(jnp.float32)
        affinity = jnp.einsum('qjd,sdk->qjsk', index_query, index_keys)
        head_rows = lax.dynamic_slice_in_dim(head_weights, start, BLK, 0)
        logits = jnp.einsum('qj,qjsk->qsk', head_rows, jnp.maximum(affinity, 0.0), precision=lax.Precision.HIGHEST)
        masked = jnp.where(valid, logits, masked_value)
        peak = jnp.max(masked, axis=(1, 2), keepdims=True)
        log_total = peak + jnp.log(jnp.sum(jnp.exp(masked - peak), axis=(1, 2), keepdims=True))
        log_probs = masked - log_total
        entropy = -jnp.sum(jnp.where(valid, target * log_probs, 0.0), axis=(1, 2))
        logit_grad = jnp.where(valid, jnp.exp(log_probs) - target, 0.0) / total_queries
        affinity_grad = (logit_grad[:, None] * head_rows[:, :, None, None] * (affinity > 0)).astype(jnp.bfloat16)
        query_grad = jnp.einsum('qjsk,sdk->qjd', affinity_grad.astype(jnp.float32), index_keys)
        return entropy, query_grad.astype(jnp.bfloat16).reshape(BLK, IH * ID)

    entropy, query_grad = lax.map(per_block, jnp.arange(QBLKS, dtype=jnp.int32))
    query_grad = query_grad.reshape(total_queries, IH * ID)
    weight_grad = jnp.einsum('td,tc->dc', index_input.astype(jnp.float32), query_grad.astype(jnp.float32))
    return weight_grad, entropy.reshape(total_queries)
```

```python
import functools

import jax
import jax.numpy as jnp
from jax import lax
from jax.experimental import pallas as pl
from jax.experimental.pallas import tpu as pltpu
from jax.sharding import Mesh, PartitionSpec as P

BF16 = jnp.bfloat16
F32 = jnp.float32
I32 = jnp.int32

H = 128
DK = 576
ID = 128
CAP = 3
BLK = 128
SEL = 16
KEYS = SEL * BLK
NY = 4
NQ = 16
SHARD = 32
LATC = DK // NY
IDXC = ID // NY
PIECE = LATC + IDXC
OWNK = KEYS // NY
HALF_COLS = 1024
IQ_ROWS = HALF_COLS + 32
LG_ROWS = OWNK + 16
DQ = 1536
COLS = HALF_COLS // NQ
QUERIES = 4096

score_scale = 192.0 ** (-0.5)
exp2_scale = score_scale * 1.4426950408889634
masked_value = -1e30
VMEM_LIMIT = 56 * 1024 * 1024

ANY = pl.BlockSpec(memory_space=pl.ANY)
VMEM = pl.BlockSpec(memory_space=pltpu.VMEM)
SMEM = pl.BlockSpec(memory_space=pltpu.SMEM)


def call(kernel, out_shape, in_specs, out_specs, scratch=(), name=None):
    return pl.pallas_call(
        kernel,
        out_shape=out_shape,
        in_specs=in_specs,
        out_specs=out_specs,
        scratch_shapes=list(scratch),
        compiler_params=pltpu.CompilerParams(vmem_limit_bytes=VMEM_LIMIT),
        name=name,
    )


def shape(dims, dtype):
    return jax.ShapeDtypeStruct(dims, dtype)


def pick_outgoing_kernel(ids, meta, cache, out, sem):
    y, core, me = meta[0], meta[1], meta[2]
    lat = pl.multiple_of(y * LATC, 16)
    idx = pl.multiple_of(DK + y * IDXC, 16)

    def copies(block, dst, slot):
        return (
            pltpu.make_async_copy(
                cache.at[block, pl.ds(lat, LATC), :], out.at[dst, slot, pl.ds(0, LATC), :], sem.at[0]
            ),
            pltpu.make_async_copy(
                cache.at[block, pl.ds(idx, IDXC), :], out.at[dst, slot, pl.ds(LATC, IDXC), :], sem.at[1]
            ),
        )

    def per_dst(dst, total):
        count = jnp.int32(0)
        for s in range(SEL):
            block = ids[2 * dst + core, s]
            mine = lax.shift_right_logical(block, 5) == me

            @pl.when(mine)
            def _(block=block, count=count):
                for c in copies(block - me * SHARD, dst, jnp.minimum(count, CAP - 1)):
                    c.start()

            count = count + mine.astype(I32)
        return total + count

    total = lax.fori_loop(0, NQ, per_dst, jnp.int32(0))

    def wait(_, carry):
        for c in copies(0, 0, 0):
            c.wait()
        return carry

    lax.fori_loop(0, total, wait, 0)


def pick_listed_kernel(ids, meta, arrived, lat, idx, seen, sem):
    core, me = meta[1], meta[2]
    row = 2 * me + core
    for i in range(NQ):
        seen[i] = 0
    pending = []
    for s in range(SEL):
        owner = lax.shift_right_logical(ids[row, s], 5)
        rank = jnp.minimum(seen[owner], CAP - 1)
        seen[owner] = seen[owner] + 1
        pending.append(
            pltpu.make_async_copy(arrived.at[owner, rank, pl.ds(LATC, IDXC), :], idx.at[s], sem.at[0])
        )
        pending.append(
            pltpu.make_async_copy(arrived.at[owner, rank, pl.ds(0, LATC), :], lat.at[s], sem.at[1])
        )
        pending[-2].start()
        pending[-1].start()
    for c in pending:
        c.wait()


def index_query_kernel(meta, x, w, hw, mine, other):
    core = meta[1]
    for k in range(4):
        cols = HALF_COLS // 4
        part = jnp.dot(x[...], w[:, k * cols : (k + 1) * cols], preferred_element_type=F32)
        part = part.astype(BF16)
        low = part[:BLK].T
        high = part[BLK:].T
        rows = pl.ds(k * cols, cols)
        first = jnp.broadcast_to(core == 0, low.shape)
        mine[rows, :] = jnp.where(first, low, high)
        other[rows, :] = jnp.where(first, high, low)
    weights = hw[...]
    hi = weights.astype(BF16)
    rest = weights - hi.astype(F32)
    mid = rest.astype(BF16)
    lo = (rest - mid.astype(F32)).astype(BF16)
    ext = jnp.concatenate(
        [hi.astype(F32), mid.astype(F32), lo.astype(F32), jnp.zeros_like(weights)], axis=0
    )
    first = jnp.broadcast_to(core == 0, (32, BLK))
    tail = pl.ds(HALF_COLS, 32)
    mine[tail, :] = jnp.where(first, ext[:, :BLK], ext[:, BLK:]).astype(BF16)
    other[tail, :] = jnp.where(first, ext[:, BLK:], ext[:, :BLK]).astype(BF16)


def head_rows(iq):
    tail = iq[HALF_COLS:, :].astype(F32)
    return tail[0:8] + tail[8:16] + tail[16:24]


def logits_kernel(meta, i0, i1, i2, i3, *rest):
    iq_refs, (logits_ref, stats_ref, keys, total) = rest[:8], rest[8:]
    y, count = meta[0], meta[3]
    for s, piece in enumerate((i0, i1, i2, i3)):
        start = pl.multiple_of(lax.rem(y + NY - s, NY) * IDXC, IDXC)
        for j in range(4):
            keys[pl.ds(start, IDXC), j * BLK : (j + 1) * BLK] = piece[4 * y + j]
    keys_t = keys[...].T
    total[...] = jnp.zeros_like(total)
    for ref in iq_refs:
        rows = head_rows(ref)
        for p in range(4):
            a, b = 2 * p, 2 * p + 1
            pair = jnp.concatenate(
                [ref[a * ID : (a + 1) * ID, :], ref[b * ID : (b + 1) * ID, :]], axis=1
            )
            affinity = jnp.maximum(jnp.dot(keys_t, pair, preferred_element_type=F32), 0.0)
            total[...] += (
                affinity[:, :BLK] * rows[a : a + 1] + affinity[:, BLK:] * rows[b : b + 1]
            )
    key = lax.broadcasted_iota(I32, (OWNK, BLK), 0) + y * OWNK
    token = lax.broadcasted_iota(I32, (OWNK, BLK), 1)
    valid = (key < count * BLK) & ((key >= BLK) | (key <= token))
    masked = jnp.where(valid, total[...], masked_value)
    logits_ref[...] = masked
    peak = jnp.max(masked, axis=0, keepdims=True)
    mass = jnp.sum(jnp.exp(masked - peak), axis=0, keepdims=True)
    row = lax.broadcasted_iota(I32, (8, BLK), 0)
    stats_ref[...] = jnp.where(row == 0, peak, mass)


def target_kernel(
    meta, l0, l1, l2, l3, q_own, q_other, o0, o1, o2, o3, keys, keys_t, qa, qb, buf_a, buf_b, total, sems
):
    y, core, count = meta[0], meta[1], meta[3]
    copies = []
    for s, piece in enumerate((l0, l1, l2, l3)):
        start = pl.multiple_of(lax.rem(y + NY - s, NY) * LATC, LATC)
        for j in range(SEL):
            copies.append(
                pltpu.make_async_copy(
                    piece.at[j], keys.at[pl.ds(start, LATC), pl.ds(j * BLK, BLK)], sems.at[0]
                )
            )
    lanes = pl.multiple_of(core * BLK, BLK)
    queries = [
        pltpu.make_async_copy(q_own.at[:, :, pl.ds(lanes, BLK)], qa, sems.at[1]),
        pltpu.make_async_copy(q_other, qb, sems.at[2]),
    ]
    for c in copies + queries:
        c.start()
    for c in copies:
        c.wait()
    for j in range(SEL):
        keys_t[j * BLK : (j + 1) * BLK, :] = keys[:, j * BLK : (j + 1) * BLK].T
    total[...] = jnp.zeros_like(total)
    for c in queries:
        c.wait()

    chunk = 256
    token = lax.broadcasted_iota(I32, (BLK, 2 * BLK), 1) % BLK
    causal = lax.broadcasted_iota(I32, (BLK, 2 * BLK), 0) <= token

    def scores(p, buf):
        pair = jnp.concatenate([qa[p], qb[p]], axis=1)
        peak = jnp.full((8, 2 * BLK), masked_value, F32)
        for k in range(KEYS // chunk):
            part = jnp.dot(
                keys_t[k * chunk : (k + 1) * chunk, :], pair, preferred_element_type=F32
            )
            for j in range(chunk // BLK):
                slot = k * (chunk // BLK) + j
                tile = part[j * BLK : (j + 1) * BLK]
                if slot == 0:
                    tile = jnp.where(causal, tile, masked_value)
                else:
                    tile = jnp.where(slot < count, tile, masked_value)
                buf[slot * BLK : (slot + 1) * BLK, :] = tile
                peak = jnp.maximum(peak, jnp.max(tile.reshape(BLK // 8, 8, 2 * BLK), axis=0))
        return jnp.max(peak, axis=0, keepdims=True)

    def spread(buf, peak):
        shift = peak * exp2_scale
        mass = jnp.zeros((8, 2 * BLK), F32)
        for j in range(SEL):
            tile = jnp.exp2(buf[j * BLK : (j + 1) * BLK, :] * exp2_scale - shift)
            buf[j * BLK : (j + 1) * BLK, :] = tile
            mass = mass + jnp.sum(tile.reshape(BLK // 8, 8, 2 * BLK), axis=0)
        share = 1.0 / (jnp.sum(mass, axis=0, keepdims=True) * H)
        for j in range(SEL):
            tile = buf[j * BLK : (j + 1) * BLK, :] * share
            total[j * BLK : (j + 1) * BLK, :] += tile[:, :BLK] + tile[:, BLK:]

    def step(k, peak_a):
        peak_b = scores(2 * k + 1, buf_b)
        spread(buf_a, peak_a)
        peak_next = scores(2 * k + 2, buf_a)
        spread(buf_b, peak_b)
        return peak_next

    pairs = qa.shape[0]
    peak_a = lax.fori_loop(0, pairs // 2 - 1, step, scores(0, buf_a))
    peak_b = scores(pairs - 1, buf_b)
    spread(buf_a, peak_a)
    spread(buf_b, peak_b)
    for s, out in enumerate((o0, o1, o2, o3)):
        start = pl.multiple_of(lax.rem(y + s, NY) * OWNK, OWNK)
        out[...] = total[pl.ds(start, OWNK), :].astype(BF16)


def loss_kernel(t0, t1, t2, t3, logits, s0, s1, s2, s3, out):
    stats = [s[...] for s in (s0, s1, s2, s3)]
    peak = functools.reduce(jnp.maximum, [s[0:1] for s in stats])
    mass = functools.reduce(jnp.add, [s[1:2] * jnp.exp(s[0:1] - peak) for s in stats])
    log_total = peak + jnp.log(mass)
    target = t0[...].astype(F32) + t1[...].astype(F32) + t2[...].astype(F32) + t3[...].astype(F32)
    masked = logits[...]
    valid = masked > 0.5 * masked_value
    log_probs = masked - log_total
    entropy = -jnp.sum(jnp.where(valid, target * log_probs, 0.0), axis=0, keepdims=True)
    grad = jnp.where(valid, jnp.exp(log_probs) - target, 0.0) / QUERIES
    out[:OWNK, :] = grad.astype(BF16)
    hi = entropy.astype(BF16).astype(F32)
    mid = (entropy - hi).astype(BF16).astype(F32)
    lo = entropy - hi - mid
    row = lax.broadcasted_iota(I32, (16, BLK), 0)
    ext = jnp.where(row == 0, hi, jnp.where(row == 1, mid, jnp.where(row == 2, lo, 0.0)))
    out[OWNK:, :] = ext.astype(BF16)


def backward_kernel(
    meta, g0, g1, g2, g3, i0, i1, i2, i3, iq0, iq1, out, entropy_ref, keys, keys_t, grads
):
    y = meta[0]
    entropy = jnp.zeros((1, BLK), F32)
    for s, piece in enumerate((g0, g1, g2, g3)):
        start = pl.multiple_of(lax.rem(y + NY - s, NY) * OWNK, OWNK)
        grads[pl.ds(start, OWNK), :] = piece[:OWNK, :].astype(F32)
        tail = piece[OWNK:, :].astype(F32)
        entropy = entropy + tail[0:1] + tail[1:2] + tail[2:3]
    entropy_ref[...] = jnp.broadcast_to(entropy, (8, BLK))
    for s, piece in enumerate((i0, i1, i2, i3)):
        start = pl.multiple_of(lax.rem(y + NY - s, NY) * IDXC, IDXC)
        for j in range(SEL):
            keys[pl.ds(start, IDXC), j * BLK : (j + 1) * BLK] = piece[j]
    for j in range(SEL):
        keys_t[j * BLK : (j + 1) * BLK, :] = keys[:, j * BLK : (j + 1) * BLK].T
    chunk = 512
    for core, ref in enumerate((iq0, iq1)):
        rows = head_rows(ref)
        for p in range(4):
            a, b = 2 * p, 2 * p + 1
            pair = jnp.concatenate(
                [ref[a * ID : (a + 1) * ID, :], ref[b * ID : (b + 1) * ID, :]], axis=1
            )
            acc = jnp.zeros((ID, 2 * BLK), F32)
            for k in range(KEYS // chunk):
                span = slice(k * chunk, (k + 1) * chunk)
                affinity = jnp.dot(keys_t[span, :], pair, preferred_element_type=F32)
                grad = grads[span, :]
                scaled = jnp.concatenate([grad * rows[a : a + 1], grad * rows[b : b + 1]], axis=1)
                masked = jnp.where(affinity > 0, scaled, 0.0).astype(BF16)
                acc = acc + jnp.dot(keys[:, span], masked, preferred_element_type=F32)
            acc = acc.astype(BF16)
            for n, head in enumerate((a, b)):
                lanes = slice(n * BLK, (n + 1) * BLK)
                out[4 * head + core] = acc[:COLS, lanes]
                out[4 * head + 2 + core] = acc[COLS:, lanes]


def weight_kernel(meta, qg, xa, xb, out, lhs, acc):
    step = pl.program_id(0)
    chunk = xa.shape[0]

    @pl.when(step == 0)
    def _():
        for s in range(2 * NQ):
            lhs[s // 4, :, (s % 4) * BLK : (s % 4 + 1) * BLK] = qg[s]
        acc[...] = jnp.zeros_like(acc)

    left = lhs[step]
    acc[0] += jnp.dot(left, xa[...], preferred_element_type=F32)
    acc[1] += jnp.dot(left, xb[...], preferred_element_type=F32)

    @pl.when(step == pl.num_programs(0) - 1)
    def _():
        own_first = jnp.broadcast_to(meta[1] == 0, acc.shape[1:])
        half = acc.shape[2]
        out[:, :half] = jnp.where(own_first, acc[0], acc[1]).astype(BF16)
        out[:, half:] = jnp.where(own_first, acc[1], acc[0]).astype(BF16)


def finish_kernel(gathered, out):
    out[...] = gathered[...].astype(F32).T


def ring(shift):
    return [(i, (i + shift) % NY) for i in range(NY)]


SWAP = [(0, 1), (1, 0)]
SHIFTS = (1, 3, 2)


def around_y(array):
    moved = {s: lax.ppermute(array, "y", ring(s)) for s in SHIFTS}
    return (array, moved[1], moved[2], moved[3])


def on_device(
    q_absorbed, key_cache, index_input, index_weight, head_weights, block_ids, block_counts
):
    y, core = lax.axis_index("y"), lax.axis_index("c")
    me = lax.axis_index(("z", "x"))
    count = lax.dynamic_index_in_dim(block_counts, 2 * me + core, 0, keepdims=False)
    meta = jnp.stack([y, core, me, count]).astype(I32)

    outgoing = call(
        pick_outgoing_kernel,
        shape((NQ, CAP, PIECE, BLK), BF16),
        [SMEM, SMEM, ANY],
        ANY,
        [pltpu.SemaphoreType.DMA((2,))],
        "pick_outgoing",
    )(block_ids, meta, key_cache)
    arrived = lax.all_to_all(outgoing, ("z", "x"), split_axis=0, concat_axis=0, tiled=True)

    iq_own, iq_send = call(
        index_query_kernel,
        (shape((IQ_ROWS, BLK), BF16),) * 2,
        [SMEM, VMEM, VMEM, VMEM],
        (VMEM, VMEM),
        name="index_query",
    )(meta, index_input, index_weight, head_weights.T)
    iq_other = lax.ppermute(iq_send, "c", SWAP)
    first = core == 0
    iq_pair = jnp.stack(
        [jnp.where(first, iq_own, iq_other), jnp.where(first, iq_other, iq_own)]
    )
    iq_all = around_y(iq_pair)

    q_t = jnp.transpose(q_absorbed, (1, 2, 0))
    q_send = lax.dynamic_slice_in_dim(q_t, (1 - core) * BLK, BLK, 2)
    q_other = lax.ppermute(q_send, "c", SWAP)

    lat, idx = call(
        pick_listed_kernel,
        (shape((SEL, LATC, BLK), BF16), shape((SEL, IDXC, BLK), BF16)),
        [SMEM, SMEM, ANY],
        (ANY, ANY),
        [pltpu.SMEM((NQ,), I32), pltpu.SemaphoreType.DMA((2,))],
        "pick_listed",
    )(block_ids, meta, arrived)
    idx_all = around_y(idx)
    lat_all = around_y(lat)

    half = DQ // 2
    x_half = lax.dynamic_slice_in_dim(index_input, core * half, half, 1)
    x_half, _ = lax.optimization_barrier((x_half, arrived))
    x_own = lax.all_gather(x_half, ("z", "x"), axis=0, tiled=True)
    x_other = lax.ppermute(x_own, "c", SWAP)

    logits, stats = call(
        logits_kernel,
        (shape((OWNK, BLK), F32), shape((8, BLK), F32)),
        [SMEM] + [VMEM] * 12,
        (VMEM, VMEM),
        [pltpu.VMEM((ID, OWNK), BF16), pltpu.VMEM((OWNK, BLK), F32)],
        "index_logits",
    )(meta, *idx_all, *[a[n] for a in iq_all for n in range(2)])
    stats_all = around_y(stats)

    targets = call(
        target_kernel,
        (shape((OWNK, BLK), BF16),) * 4,
        [SMEM] + [ANY] * 6,
        (VMEM,) * 4,
        [
            pltpu.VMEM((DK, KEYS), BF16),
            pltpu.VMEM((KEYS, DK), BF16),
            pltpu.VMEM((16, DK, BLK), BF16),
            pltpu.VMEM((16, DK, BLK), BF16),
            pltpu.VMEM((KEYS, 2 * BLK), F32),
            pltpu.VMEM((KEYS, 2 * BLK), F32),
            pltpu.VMEM((KEYS, BLK), F32),
            pltpu.SemaphoreType.DMA((3,)),
        ],
        "attention_target",
    )(meta, *lat_all, q_t, q_other)
    arrived_targets = {s: lax.ppermute(targets[s], "y", ring(s)) for s in SHIFTS}

    grads = call(
        loss_kernel,
        shape((LG_ROWS, BLK), BF16),
        [VMEM] * 9,
        VMEM,
        name="loss",
    )(targets[0], arrived_targets[1], arrived_targets[2], arrived_targets[3], logits, *stats_all)
    grads_all = around_y(grads)

    query_grad, entropy = call(
        backward_kernel,
        (shape((2 * NQ, COLS, BLK), BF16), shape((8, BLK), F32)),
        [SMEM] + [VMEM] * 10,
        (VMEM, VMEM),
        [
            pltpu.VMEM((ID, KEYS), BF16),
            pltpu.VMEM((KEYS, ID), BF16),
            pltpu.VMEM((KEYS, BLK), F32),
        ],
        "index_backward",
    )(meta, *grads_all, *idx_all, iq_pair[0], iq_pair[1])
    entropy_other = lax.ppermute(entropy, "c", SWAP)
    entropy_both = jnp.where(
        first,
        jnp.concatenate([entropy[0], entropy_other[0]]),
        jnp.concatenate([entropy_other[0], entropy[0]]),
    )
    share = 2 * BLK // (2 * NY)
    entropy_mine = lax.dynamic_slice_in_dim(entropy_both, (2 * y + core) * share, share, 0)

    swapped = lax.all_to_all(query_grad, ("z", "x", "c"), split_axis=0, concat_axis=0, tiled=True)
    chunk = 512
    piece = pl.pallas_call(
        weight_kernel,
        grid=(QUERIES // chunk,),
        out_shape=shape((COLS, DQ), BF16),
        in_specs=[
            SMEM,
            pl.BlockSpec((2 * NQ, COLS, BLK), lambda i: (0, 0, 0)),
            pl.BlockSpec((chunk, half), lambda i: (i, 0)),
            pl.BlockSpec((chunk, half), lambda i: (i, 0)),
        ],
        out_specs=pl.BlockSpec((COLS, DQ), lambda i: (0, 0)),
        scratch_shapes=[
            pltpu.VMEM((QUERIES // chunk, COLS, chunk), BF16),
            pltpu.VMEM((2, COLS, half), F32),
        ],
        compiler_params=pltpu.CompilerParams(vmem_limit_bytes=VMEM_LIMIT),
        name="weight_piece",
    )(meta, swapped, x_own, x_other)
    gathered = lax.all_gather(piece, ("z", "x"), axis=0, tiled=True)
    weight_grad = pl.pallas_call(
        finish_kernel,
        grid=(6,),
        out_shape=shape((DQ, HALF_COLS), F32),
        in_specs=[pl.BlockSpec((HALF_COLS, 256), lambda i: (0, i))],
        out_specs=pl.BlockSpec((256, HALF_COLS), lambda i: (i, 0)),
        compiler_params=pltpu.CompilerParams(vmem_limit_bytes=VMEM_LIMIT),
        name="finish",
    )(gathered)
    return weight_grad, entropy_mine


def solution(mesh):
    fine = Mesh(mesh.devices.reshape(NY, 2, 4, 4), ("y", "c", "z", "x"))
    head, qblk = ("y", "c"), ("z", "x")
    placed = (
        P(qblk, head, None),
        P(qblk, None, None),
        P(qblk, None),
        P(None, head),
        P(qblk, head),
        P(),
        P(),
    )
    return jax.shard_map(
        on_device,
        mesh=fine,
        in_specs=placed,
        out_specs=(P(None, head), P(qblk + head)),
        check_vma=False,
    )
```

```python
import functools

import jax
import jax.numpy as jnp
from jax import lax
from jax.experimental import pallas as pl
from jax.experimental.pallas import tpu as pltpu
from jax.sharding import Mesh, PartitionSpec as P

BF16 = jnp.bfloat16
F32 = jnp.float32
I32 = jnp.int32

H = 128
DK = 576
ID = 128
CAP = 3
BLK = 128
SEL = 16
KEYS = SEL * BLK
NY = 4
NQ = 16
SHARD = 32
LATC = DK // NY
IDXC = ID // NY
PIECE = LATC + IDXC
OWNK = KEYS // NY
HALF_COLS = 1024
IQ_ROWS = HALF_COLS + 32
LG_ROWS = OWNK + 16
DQ = 1536
COLS = HALF_COLS // NQ
QUERIES = 4096

score_scale = 192.0 ** (-0.5)
exp2_scale = score_scale * 1.4426950408889634
masked_value = -1e30
VMEM_LIMIT = 56 * 1024 * 1024

ANY = pl.BlockSpec(memory_space=pl.ANY)
VMEM = pl.BlockSpec(memory_space=pltpu.VMEM)
SMEM = pl.BlockSpec(memory_space=pltpu.SMEM)


def call(kernel, out_shape, in_specs, out_specs, scratch=(), name=None):
    return pl.pallas_call(
        kernel,
        out_shape=out_shape,
        in_specs=in_specs,
        out_specs=out_specs,
        scratch_shapes=list(scratch),
        compiler_params=pltpu.CompilerParams(vmem_limit_bytes=VMEM_LIMIT),
        name=name,
    )


def shape(dims, dtype):
    return jax.ShapeDtypeStruct(dims, dtype)


def place():
    return lax.axis_index("y"), lax.axis_index("c"), lax.axis_index(("z", "x"))


def slots_in_use(counts):
    _, core, me = place()
    return counts[2 * me + core]


def pick_outgoing_kernel(ids, cache, out, sem):
    y, core, me = place()
    lat = pl.multiple_of(y * LATC, 16)
    idx = pl.multiple_of(DK + y * IDXC, 16)

    def copies(block, dst, slot):
        return (
            pltpu.make_async_copy(
                cache.at[block, pl.ds(lat, LATC), :], out.at[dst, slot, pl.ds(0, LATC), :], sem.at[0]
            ),
            pltpu.make_async_copy(
                cache.at[block, pl.ds(idx, IDXC), :], out.at[dst, slot, pl.ds(LATC, IDXC), :], sem.at[1]
            ),
        )

    def per_dst(dst, total):
        count = jnp.int32(0)
        for s in range(SEL):
            block = ids[s, 2 * dst + core]
            mine = lax.shift_right_logical(block, 5) == me

            @pl.when(mine)
            def _(block=block, count=count):
                for c in copies(block - me * SHARD, dst, jnp.minimum(count, CAP - 1)):
                    c.start()

            count = count + mine.astype(I32)
        return total + count

    total = lax.fori_loop(0, NQ, per_dst, jnp.int32(0))

    def wait(_, carry):
        for c in copies(0, 0, 0):
            c.wait()
        return carry

    lax.fori_loop(0, total, wait, 0)


def pick_listed_kernel(ids, arrived, *refs):
    lat, idx, seen, sem = refs[-4:]
    _, core, me = place()
    row = 2 * me + core
    for i in range(NQ):
        seen[i] = 0
    pending = []
    for s in range(SEL):
        owner = lax.shift_right_logical(ids[s, row], 5)
        rank = jnp.minimum(seen[owner], CAP - 1)
        seen[owner] = seen[owner] + 1
        pending.append(
            pltpu.make_async_copy(arrived.at[owner, rank, pl.ds(LATC, IDXC), :], idx.at[s], sem.at[0])
        )
        pending.append(
            pltpu.make_async_copy(arrived.at[owner, rank, pl.ds(0, LATC), :], lat.at[s], sem.at[1])
        )
        pending[-2].start()
        pending[-1].start()
    for c in pending:
        c.wait()


def index_query_kernel(x, w, hw, mine, other):
    core = lax.axis_index("c")
    for k in range(4):
        cols = HALF_COLS // 4
        part = jnp.dot(x[...], w[:, k * cols : (k + 1) * cols], preferred_element_type=F32)
        part = part.astype(BF16)
        low = part[:BLK].T
        high = part[BLK:].T
        rows = pl.ds(k * cols, cols)
        first = jnp.broadcast_to(core == 0, low.shape)
        mine[rows, :] = jnp.where(first, low, high)
        other[rows, :] = jnp.where(first, high, low)
    weights = hw[...]
    hi = weights.astype(BF16)
    rest = weights - hi.astype(F32)
    mid = rest.astype(BF16)
    lo = (rest - mid.astype(F32)).astype(BF16)
    ext = jnp.concatenate(
        [hi.astype(F32), mid.astype(F32), lo.astype(F32), jnp.zeros_like(weights)], axis=0
    )
    first = jnp.broadcast_to(core == 0, (32, BLK))
    tail = pl.ds(HALF_COLS, 32)
    mine[tail, :] = jnp.where(first, ext[:, :BLK], ext[:, BLK:]).astype(BF16)
    other[tail, :] = jnp.where(first, ext[:, BLK:], ext[:, :BLK]).astype(BF16)


def head_rows(tail):
    tail = tail.astype(F32)
    return tail[0:8] + tail[8:16] + tail[16:24]


def logits_kernel(counts, i0, i1, i2, i3, *rest):
    iq_refs, (logits_ref, stats_ref, keys, total) = rest[:4], rest[4:]
    y, count = lax.axis_index("y"), slots_in_use(counts)
    for s, piece in enumerate((i0, i1, i2, i3)):
        start = pl.multiple_of(lax.rem(y + NY - s, NY) * IDXC, IDXC)
        for j in range(4):
            keys[pl.ds(start, IDXC), j * BLK : (j + 1) * BLK] = piece[4 * y + j]
    keys_t = keys[...].T
    total[...] = jnp.zeros_like(total)
    for ref in [r.at[n] for r in iq_refs for n in range(2)]:
        rows = head_rows(ref[HALF_COLS:, :])
        for p in range(4):
            a, b = 2 * p, 2 * p + 1
            pair = jnp.concatenate(
                [ref[a * ID : (a + 1) * ID, :], ref[b * ID : (b + 1) * ID, :]], axis=1
            )
            affinity = jnp.maximum(jnp.dot(keys_t, pair, preferred_element_type=F32), 0.0)
            total[...] += (
                affinity[:, :BLK] * rows[a : a + 1] + affinity[:, BLK:] * rows[b : b + 1]
            )
    key = lax.broadcasted_iota(I32, (OWNK, BLK), 0) + y * OWNK
    token = lax.broadcasted_iota(I32, (OWNK, BLK), 1)
    valid = (key < count * BLK) & ((key >= BLK) | (key <= token))
    masked = jnp.where(valid, total[...], masked_value)
    logits_ref[...] = masked
    peak = jnp.max(masked, axis=0, keepdims=True)
    mass = jnp.sum(jnp.exp(masked - peak), axis=0, keepdims=True)
    row = lax.broadcasted_iota(I32, (8, BLK), 0)
    stats_ref[...] = jnp.where(row == 0, peak, mass)


def split_rows(row):
    hi = row.astype(BF16).astype(F32)
    mid = (row - hi).astype(BF16).astype(F32)
    return hi, mid, row - hi - mid


def tail_tile(rows):
    at = lax.broadcasted_iota(I32, (16, BLK), 0)
    tile = jnp.zeros((16, BLK), F32)
    for n, row in enumerate(rows):
        tile = jnp.where(at == n, row, tile)
    return tile.astype(BF16)


def target_kernel(
    counts, stats, l0, l1, l2, l3, q_own, q_other, o0, o1, o2, o3, keys, keys_t, qa, qb, buf_a, buf_b, total, sems
):
    y, core, _ = place()
    count = slots_in_use(counts)
    copies = []
    for s, piece in enumerate((l0, l1, l2, l3)):
        start = pl.multiple_of(lax.rem(y + NY - s, NY) * LATC, LATC)
        for j in range(SEL):
            copies.append(
                pltpu.make_async_copy(
                    piece.at[j], keys.at[pl.ds(start, LATC), pl.ds(j * BLK, BLK)], sems.at[0]
                )
            )
    lanes = pl.multiple_of(core * BLK, BLK)
    queries = [
        pltpu.make_async_copy(q_own.at[:, :, pl.ds(lanes, BLK)], qa, sems.at[1]),
        pltpu.make_async_copy(q_other, qb, sems.at[2]),
    ]
    for c in copies + queries:
        c.start()
    for c in copies:
        c.wait()
    for j in range(SEL):
        keys_t[j * BLK : (j + 1) * BLK, :] = keys[:, j * BLK : (j + 1) * BLK].T
    total[...] = jnp.zeros_like(total)
    for c in queries:
        c.wait()

    chunk = 256
    token = lax.broadcasted_iota(I32, (BLK, 2 * BLK), 1) % BLK
    causal = lax.broadcasted_iota(I32, (BLK, 2 * BLK), 0) <= token

    def scores(p, buf):
        pair = jnp.concatenate([qa[p], qb[p]], axis=1)
        peak = jnp.full((8, 2 * BLK), masked_value, F32)
        for k in range(KEYS // chunk):
            part = jnp.dot(
                keys_t[k * chunk : (k + 1) * chunk, :], pair, preferred_element_type=F32
            )
            for j in range(chunk // BLK):
                slot = k * (chunk // BLK) + j
                tile = part[j * BLK : (j + 1) * BLK]
                if slot == 0:
                    tile = jnp.where(causal, tile, masked_value)
                else:
                    tile = jnp.where(slot < count, tile, masked_value)
                buf[slot * BLK : (slot + 1) * BLK, :] = tile
                peak = jnp.maximum(peak, jnp.max(tile.reshape(BLK // 8, 8, 2 * BLK), axis=0))
        return jnp.max(peak, axis=0, keepdims=True)

    def spread(buf, peak):
        shift = peak * exp2_scale
        mass = jnp.zeros((8, 2 * BLK), F32)
        for j in range(SEL):
            tile = jnp.exp2(buf[j * BLK : (j + 1) * BLK, :] * exp2_scale - shift)
            buf[j * BLK : (j + 1) * BLK, :] = tile
            mass = mass + jnp.sum(tile.reshape(BLK // 8, 8, 2 * BLK), axis=0)
        share = 1.0 / (jnp.sum(mass, axis=0, keepdims=True) * H)
        for j in range(SEL):
            tile = buf[j * BLK : (j + 1) * BLK, :] * share
            total[j * BLK : (j + 1) * BLK, :] += tile[:, :BLK] + tile[:, BLK:]

    def step(k, peak_a):
        peak_b = scores(2 * k + 1, buf_b)
        spread(buf_a, peak_a)
        peak_next = scores(2 * k + 2, buf_a)
        spread(buf_b, peak_b)
        return peak_next

    pairs = qa.shape[0]
    peak_a = lax.fori_loop(0, pairs // 2 - 1, step, scores(0, buf_a))
    peak_b = scores(pairs - 1, buf_b)
    spread(buf_a, peak_a)
    spread(buf_b, peak_b)
    tail = tail_tile(split_rows(stats[0:1, :]) + split_rows(stats[1:2, :]))
    for s, out in enumerate((o0, o1, o2, o3)):
        start = pl.multiple_of(lax.rem(y + s, NY) * OWNK, OWNK)
        out[:OWNK, :] = total[pl.ds(start, OWNK), :].astype(BF16)
        out[OWNK:, :] = tail


def loss_kernel(t0, t1, t2, t3, logits, out):
    pieces = (t0, t1, t2, t3)
    tails = [t[OWNK:, :].astype(F32) for t in pieces]
    peaks = [t[0:1] + t[1:2] + t[2:3] for t in tails]
    masses = [t[3:4] + t[4:5] + t[5:6] for t in tails]
    peak = functools.reduce(jnp.maximum, peaks)
    mass = functools.reduce(jnp.add, [m * jnp.exp(p - peak) for m, p in zip(masses, peaks)])
    log_total = peak + jnp.log(mass)
    target = functools.reduce(jnp.add, [t[:OWNK, :].astype(F32) for t in pieces])
    masked = logits[...]
    valid = masked > 0.5 * masked_value
    log_probs = masked - log_total
    entropy = -jnp.sum(jnp.where(valid, target * log_probs, 0.0), axis=0, keepdims=True)
    grad = jnp.where(valid, jnp.exp(log_probs) - target, 0.0) / QUERIES
    out[:OWNK, :] = grad.astype(BF16)
    out[OWNK:, :] = tail_tile(split_rows(entropy))


def backward_kernel(
    g0, g1, g2, g3, i0, i1, i2, i3, iq, out, entropy_ref, keys, keys_t, grads
):
    y = lax.axis_index("y")
    entropy = jnp.zeros((1, BLK), F32)
    for s, piece in enumerate((g0, g1, g2, g3)):
        start = pl.multiple_of(lax.rem(y + NY - s, NY) * OWNK, OWNK)
        grads[pl.ds(start, OWNK), :] = piece[:OWNK, :].astype(F32)
        tail = piece[OWNK:, :].astype(F32)
        entropy = entropy + tail[0:1] + tail[1:2] + tail[2:3]
    entropy_ref[...] = jnp.broadcast_to(entropy, (8, BLK))
    for s, piece in enumerate((i0, i1, i2, i3)):
        start = pl.multiple_of(lax.rem(y + NY - s, NY) * IDXC, IDXC)
        for j in range(SEL):
            keys[pl.ds(start, IDXC), j * BLK : (j + 1) * BLK] = piece[j]
    for j in range(SEL):
        keys_t[j * BLK : (j + 1) * BLK, :] = keys[:, j * BLK : (j + 1) * BLK].T
    chunk = 512
    for core in range(2):
        ref = iq.at[core]
        rows = head_rows(ref[HALF_COLS:, :])
        for p in range(4):
            a, b = 2 * p, 2 * p + 1
            pair = jnp.concatenate(
                [ref[a * ID : (a + 1) * ID, :], ref[b * ID : (b + 1) * ID, :]], axis=1
            )
            acc = jnp.zeros((ID, 2 * BLK), F32)
            for k in range(KEYS // chunk):
                span = slice(k * chunk, (k + 1) * chunk)
                affinity = jnp.dot(keys_t[span, :], pair, preferred_element_type=F32)
                grad = grads[span, :]
                scaled = jnp.concatenate([grad * rows[a : a + 1], grad * rows[b : b + 1]], axis=1)
                masked = jnp.where(affinity > 0, scaled, 0.0).astype(BF16)
                acc = acc + jnp.dot(keys[:, span], masked, preferred_element_type=F32)
            acc = acc.astype(BF16)
            for n, head in enumerate((a, b)):
                lanes = slice(n * BLK, (n + 1) * BLK)
                out[4 * head + core] = acc[:COLS, lanes]
                out[4 * head + 2 + core] = acc[COLS:, lanes]


def weight_kernel(qg, xa, xb, out, lhs, acc):
    step = pl.program_id(0)
    chunk = xa.shape[0]

    @pl.when(step == 0)
    def _():
        for s in range(2 * NQ):
            lhs[s // 4, :, (s % 4) * BLK : (s % 4 + 1) * BLK] = qg[s]
        acc[...] = jnp.zeros_like(acc)

    left = lhs[step]
    acc[0] += jnp.dot(left, xa[...], preferred_element_type=F32)
    acc[1] += jnp.dot(left, xb[...], preferred_element_type=F32)

    @pl.when(step == pl.num_programs(0) - 1)
    def _():
        own_first = jnp.broadcast_to(lax.axis_index("c") == 0, acc.shape[1:])
        half = acc.shape[2]
        out[:, :half] = jnp.where(own_first, acc[0], acc[1]).astype(BF16)
        out[:, half:] = jnp.where(own_first, acc[1], acc[0]).astype(BF16)


def finish_kernel(gathered, out):
    out[...] = gathered[...].astype(F32).T


def ring(shift):
    return [(i, (i + shift) % NY) for i in range(NY)]


SWAP = [(0, 1), (1, 0)]
SHIFTS = (1, 3, 2)


def around_y(array):
    moved = {s: lax.ppermute(array, "y", ring(s)) for s in SHIFTS}
    return (array, moved[1], moved[2], moved[3])


def on_device(
    q_absorbed, key_cache, index_input, index_weight, head_weights, block_ids, block_counts
):
    y, core, _ = place()
    ids = block_ids.T

    outgoing = call(
        pick_outgoing_kernel,
        shape((NQ, CAP, PIECE, BLK), BF16),
        [SMEM, ANY],
        VMEM,
        [pltpu.SemaphoreType.DMA((2,))],
        "pick_outgoing",
    )(ids, key_cache)
    arrived = lax.all_to_all(outgoing, ("z", "x"), split_axis=0, concat_axis=0, tiled=True)

    iq_own, iq_send = call(
        index_query_kernel,
        (shape((IQ_ROWS, BLK), BF16),) * 2,
        [VMEM, VMEM, VMEM],
        (VMEM, VMEM),
        name="index_query",
    )(index_input, index_weight, head_weights.T)
    iq_other = lax.ppermute(iq_send, "c", SWAP)
    first = core == 0
    iq_pair = jnp.stack(
        [jnp.where(first, iq_own, iq_other), jnp.where(first, iq_other, iq_own)]
    )
    iq_all = around_y(iq_pair)

    q_t = jnp.transpose(q_absorbed, (1, 2, 0))
    q_send = lax.dynamic_slice_in_dim(q_t, (1 - core) * BLK, BLK, 2)
    q_other = lax.ppermute(q_send, "c", SWAP)

    lat, idx = call(
        pick_listed_kernel,
        (shape((SEL, LATC, BLK), BF16), shape((SEL, IDXC, BLK), BF16)),
        [SMEM] + [ANY] * 5,
        (VMEM, VMEM),
        [pltpu.SMEM((NQ,), I32), pltpu.SemaphoreType.DMA((2,))],
        "pick_listed",
    )(ids, arrived, q_send, *iq_all[1:])
    idx_all = around_y(idx)
    lat = lax.optimization_barrier((lat, *idx_all[1:]))[0]
    lat_all = around_y(lat)

    half = DQ // 2
    x_half = lax.dynamic_slice_in_dim(index_input, core * half, half, 1)
    x_half, _ = lax.optimization_barrier((x_half, idx))
    x_own = lax.all_gather(x_half, ("z", "x"), axis=0, tiled=True)

    logits, stats = call(
        logits_kernel,
        (shape((OWNK, BLK), F32), shape((8, BLK), F32)),
        [SMEM] + [VMEM] * 8,
        (VMEM, VMEM),
        [pltpu.VMEM((ID, OWNK), BF16), pltpu.VMEM((OWNK, BLK), F32)],
        "index_logits",
    )(block_counts, *idx_all, *iq_all)

    targets = call(
        target_kernel,
        (shape((LG_ROWS, BLK), BF16),) * 4,
        [SMEM, VMEM] + [ANY] * 6,
        (VMEM,) * 4,
        [
            pltpu.VMEM((DK, KEYS), BF16),
            pltpu.VMEM((KEYS, DK), BF16),
            pltpu.VMEM((16, DK, BLK), BF16),
            pltpu.VMEM((16, DK, BLK), BF16),
            pltpu.VMEM((KEYS, 2 * BLK), F32),
            pltpu.VMEM((KEYS, 2 * BLK), F32),
            pltpu.VMEM((KEYS, BLK), F32),
            pltpu.SemaphoreType.DMA((3,)),
        ],
        "attention_target",
    )(block_counts, stats, *lat_all, q_t, q_other)
    x_own, _ = lax.optimization_barrier((x_own, targets[0]))
    x_other = lax.ppermute(x_own, "c", SWAP)
    arrived_targets = {s: lax.ppermute(targets[s], "y", ring(s)) for s in SHIFTS}

    grads = call(
        loss_kernel,
        shape((LG_ROWS, BLK), BF16),
        [VMEM] * 5,
        VMEM,
        name="loss",
    )(targets[0], arrived_targets[1], arrived_targets[2], arrived_targets[3], logits)
    grads_all = around_y(grads)

    query_grad, entropy = call(
        backward_kernel,
        (shape((2 * NQ, COLS, BLK), BF16), shape((8, BLK), F32)),
        [VMEM] * 9,
        (VMEM, VMEM),
        [
            pltpu.VMEM((ID, KEYS), BF16),
            pltpu.VMEM((KEYS, ID), BF16),
            pltpu.VMEM((KEYS, BLK), F32),
        ],
        "index_backward",
    )(*grads_all, *idx_all, iq_pair)
    entropy_other = lax.ppermute(entropy, "c", SWAP)
    entropy_both = jnp.where(
        first,
        jnp.concatenate([entropy[0], entropy_other[0]]),
        jnp.concatenate([entropy_other[0], entropy[0]]),
    )
    share = 2 * BLK // (2 * NY)
    entropy_mine = lax.dynamic_slice_in_dim(entropy_both, (2 * y + core) * share, share, 0)

    swapped = lax.all_to_all(query_grad, ("z", "x", "c"), split_axis=0, concat_axis=0, tiled=True)
    chunk = 512
    piece = pl.pallas_call(
        weight_kernel,
        grid=(QUERIES // chunk,),
        out_shape=shape((COLS, DQ), BF16),
        in_specs=[
            pl.BlockSpec((2 * NQ, COLS, BLK), lambda i: (0, 0, 0)),
            pl.BlockSpec((chunk, half), lambda i: (i, 0)),
            pl.BlockSpec((chunk, half), lambda i: (i, 0)),
        ],
        out_specs=pl.BlockSpec((COLS, DQ), lambda i: (0, 0)),
        scratch_shapes=[
            pltpu.VMEM((QUERIES // chunk, COLS, chunk), BF16),
            pltpu.VMEM((2, COLS, half), F32),
        ],
        compiler_params=pltpu.CompilerParams(vmem_limit_bytes=VMEM_LIMIT),
        name="weight_piece",
    )(swapped, x_own, x_other)
    gathered = lax.all_gather(piece, ("z", "x"), axis=0, tiled=True)
    weight_grad = pl.pallas_call(
        finish_kernel,
        grid=(6,),
        out_shape=shape((DQ, HALF_COLS), F32),
        in_specs=[pl.BlockSpec((HALF_COLS, 256), lambda i: (0, i))],
        out_specs=pl.BlockSpec((256, HALF_COLS), lambda i: (i, 0)),
        compiler_params=pltpu.CompilerParams(vmem_limit_bytes=VMEM_LIMIT),
        name="finish",
    )(gathered)
    return weight_grad, entropy_mine


def solution(mesh):
    fine = Mesh(mesh.devices.reshape(NY, 2, 4, 4), ("y", "c", "z", "x"))
    head, qblk = ("y", "c"), ("z", "x")
    placed = (
        P(qblk, head, None),
        P(qblk, None, None),
        P(qblk, None),
        P(None, head),
        P(qblk, head),
        P(),
        P(),
    )
    return jax.shard_map(
        on_device,
        mesh=fine,
        in_specs=placed,
        out_specs=(P(None, head), P(qblk + head)),
        check_vma=False,
    )
```

```python
import functools

import jax
import jax.numpy as jnp
from jax import lax
from jax.experimental import pallas as pl
from jax.experimental.pallas import tpu as pltpu
from jax.sharding import Mesh, PartitionSpec as P

BF16 = jnp.bfloat16
F32 = jnp.float32
I32 = jnp.int32

H = 128
DK = 576
ID = 128
CAP = 3
BLK = 128
SEL = 16
KEYS = SEL * BLK
NY = 4
NQ = 16
SHARD = 32
LATC = DK // NY
IDXC = ID // NY
PIECE = LATC + IDXC
OWNK = KEYS // NY
HALF_COLS = 1024
IQ_ROWS = HALF_COLS + 32
LG_ROWS = OWNK + 16
DQ = 1536
COLS = HALF_COLS // NQ
QUERIES = 4096

score_scale = 192.0 ** (-0.5)
exp2_scale = score_scale * 1.4426950408889634
masked_value = -1e30
VMEM_LIMIT = 40 * 1024 * 1024

ANY = pl.BlockSpec(memory_space=pl.ANY)
VMEM = pl.BlockSpec(memory_space=pltpu.VMEM)
SMEM = pl.BlockSpec(memory_space=pltpu.SMEM)


def call(kernel, out_shape, in_specs, out_specs, scratch=(), name=None):
    return pl.pallas_call(
        kernel,
        out_shape=out_shape,
        in_specs=in_specs,
        out_specs=out_specs,
        scratch_shapes=list(scratch),
        compiler_params=pltpu.CompilerParams(vmem_limit_bytes=VMEM_LIMIT),
        name=name,
    )


def shape(dims, dtype):
    return jax.ShapeDtypeStruct(dims, dtype)


def in_hbm(array):
    return pltpu.with_memory_space_constraint(array, pltpu.HBM)


def in_vmem(array):
    return pltpu.with_memory_space_constraint(array, pltpu.VMEM)


def place():
    return lax.axis_index("y"), lax.axis_index("c"), lax.axis_index(("z", "x"))


def slots_in_use(counts):
    _, core, me = place()
    return counts[2 * me + core]


def pick_outgoing_kernel(ids, cache, out, sem):
    y, core, me = place()
    lat = pl.multiple_of(y * LATC, 16)
    idx = pl.multiple_of(DK + y * IDXC, 16)

    def copies(block, dst, slot):
        return (
            pltpu.make_async_copy(
                cache.at[block, pl.ds(lat, LATC), :], out.at[dst, slot, pl.ds(0, LATC), :], sem.at[0]
            ),
            pltpu.make_async_copy(
                cache.at[block, pl.ds(idx, IDXC), :], out.at[dst, slot, pl.ds(LATC, IDXC), :], sem.at[1]
            ),
        )

    def per_dst(dst, total):
        count = jnp.int32(0)
        for s in range(SEL):
            block = ids[s, 2 * dst + core]
            mine = lax.shift_right_logical(block, 5) == me

            @pl.when(mine)
            def _(block=block, count=count):
                for c in copies(block - me * SHARD, dst, jnp.minimum(count, CAP - 1)):
                    c.start()

            count = count + mine.astype(I32)
        return total + count

    total = lax.fori_loop(0, NQ, per_dst, jnp.int32(0))

    def wait(_, carry):
        for c in copies(0, 0, 0):
            c.wait()
        return carry

    lax.fori_loop(0, total, wait, 0)


def pick_listed_kernel(ids, arrived, *refs):
    lat, idx, seen, sem = refs[-4:]
    _, core, me = place()
    row = 2 * me + core
    for i in range(NQ):
        seen[i] = 0
    pending = []
    for s in range(SEL):
        owner = lax.shift_right_logical(ids[s, row], 5)
        rank = jnp.minimum(seen[owner], CAP - 1)
        seen[owner] = seen[owner] + 1
        pending.append(
            pltpu.make_async_copy(arrived.at[owner, rank, pl.ds(LATC, IDXC), :], idx.at[s], sem.at[0])
        )
        pending.append(
            pltpu.make_async_copy(arrived.at[owner, rank, pl.ds(0, LATC), :], lat.at[s], sem.at[1])
        )
        pending[-2].start()
        pending[-1].start()
    for c in pending:
        c.wait()


def index_query_kernel(x, w, hw, mine, other):
    core = lax.axis_index("c")
    for k in range(4):
        cols = HALF_COLS // 4
        part = jnp.dot(x[...], w[:, k * cols : (k + 1) * cols], preferred_element_type=F32)
        part = part.astype(BF16)
        low = part[:BLK].T
        high = part[BLK:].T
        rows = pl.ds(k * cols, cols)
        first = jnp.broadcast_to(core == 0, low.shape)
        mine[rows, :] = jnp.where(first, low, high)
        other[rows, :] = jnp.where(first, high, low)
    weights = hw[...]
    hi = weights.astype(BF16)
    rest = weights - hi.astype(F32)
    mid = rest.astype(BF16)
    lo = (rest - mid.astype(F32)).astype(BF16)
    ext = jnp.concatenate(
        [hi.astype(F32), mid.astype(F32), lo.astype(F32), jnp.zeros_like(weights)], axis=0
    )
    first = jnp.broadcast_to(core == 0, (32, BLK))
    tail = pl.ds(HALF_COLS, 32)
    mine[tail, :] = jnp.where(first, ext[:, :BLK], ext[:, BLK:]).astype(BF16)
    other[tail, :] = jnp.where(first, ext[:, BLK:], ext[:, :BLK]).astype(BF16)


def head_rows(tail):
    tail = tail.astype(F32)
    return tail[0:8] + tail[8:16] + tail[16:24]


def logits_kernel(counts, i0, i1, i2, i3, *rest):
    iq_refs, (logits_ref, stats_ref, keys, total) = rest[:4], rest[4:]
    y, count = lax.axis_index("y"), slots_in_use(counts)
    for s, piece in enumerate((i0, i1, i2, i3)):
        start = pl.multiple_of(lax.rem(y + NY - s, NY) * IDXC, IDXC)
        for j in range(4):
            keys[pl.ds(start, IDXC), j * BLK : (j + 1) * BLK] = piece[4 * y + j]
    keys_t = keys[...].T
    total[...] = jnp.zeros_like(total)
    for ref in [r.at[n] for r in iq_refs for n in range(2)]:
        rows = head_rows(ref[HALF_COLS:, :])
        for p in range(4):
            a, b = 2 * p, 2 * p + 1
            pair = jnp.concatenate(
                [ref[a * ID : (a + 1) * ID, :], ref[b * ID : (b + 1) * ID, :]], axis=1
            )
            affinity = jnp.maximum(jnp.dot(keys_t, pair, preferred_element_type=F32), 0.0)
            total[...] += (
                affinity[:, :BLK] * rows[a : a + 1] + affinity[:, BLK:] * rows[b : b + 1]
            )
    key = lax.broadcasted_iota(I32, (OWNK, BLK), 0) + y * OWNK
    token = lax.broadcasted_iota(I32, (OWNK, BLK), 1)
    valid = (key < count * BLK) & ((key >= BLK) | (key <= token))
    masked = jnp.where(valid, total[...], masked_value)
    logits_ref[...] = masked
    peak = jnp.max(masked, axis=0, keepdims=True)
    mass = jnp.sum(jnp.exp(masked - peak), axis=0, keepdims=True)
    row = lax.broadcasted_iota(I32, (8, BLK), 0)
    stats_ref[...] = jnp.where(row == 0, peak, mass)


def split_rows(row):
    hi = row.astype(BF16).astype(F32)
    mid = (row - hi).astype(BF16).astype(F32)
    return hi, mid, row - hi - mid


def tail_tile(rows):
    at = lax.broadcasted_iota(I32, (16, BLK), 0)
    tile = jnp.zeros((16, BLK), F32)
    for n, row in enumerate(rows):
        tile = jnp.where(at == n, row, tile)
    return tile.astype(BF16)


def target_kernel(
    counts, stats, l0, l1, l2, l3, q_own, qb, o0, o1, o2, o3, keys, keys_t, qa, buf_a, buf_b, total, sems
):
    y, core, _ = place()
    count = slots_in_use(counts)
    copies = []
    for s, piece in enumerate((l0, l1, l2, l3)):
        start = pl.multiple_of(lax.rem(y + NY - s, NY) * LATC, LATC)
        for j in range(SEL):
            copies.append(
                pltpu.make_async_copy(
                    piece.at[j], keys.at[pl.ds(start, LATC), pl.ds(j * BLK, BLK)], sems.at[0]
                )
            )
    lanes = pl.multiple_of(core * BLK, BLK)
    queries = [
        pltpu.make_async_copy(q_own.at[:, :, pl.ds(lanes, BLK)], qa, sems.at[1]),
    ]
    for c in copies + queries:
        c.start()
    for c in copies:
        c.wait()
    for j in range(SEL):
        keys_t[j * BLK : (j + 1) * BLK, :] = keys[:, j * BLK : (j + 1) * BLK].T
    total[...] = jnp.zeros_like(total)
    for c in queries:
        c.wait()

    chunk = 512
    token = lax.broadcasted_iota(I32, (BLK, 2 * BLK), 1) % BLK
    causal = lax.broadcasted_iota(I32, (BLK, 2 * BLK), 0) <= token

    def rows_of(tile):
        return tile.reshape(tile.shape[0] // 8, 8, 2 * BLK)

    def score_part(pair, buf, k, peak):
        part = jnp.dot(keys_t[k * chunk : (k + 1) * chunk, :], pair, preferred_element_type=F32)
        for j in range(chunk // BLK):
            slot = k * (chunk // BLK) + j
            tile = part[j * BLK : (j + 1) * BLK]
            if slot == 0:
                tile = jnp.where(causal, tile, masked_value)
            buf[slot * BLK : (slot + 1) * BLK, :] = tile
            top = jnp.max(rows_of(tile), axis=0)
            peak = jnp.maximum(peak, jnp.where(slot < count, top, masked_value))
        return peak

    def exp_part(buf, k, shift, mass):
        span = slice(k * BLK, (k + 1) * BLK)
        tile = jnp.exp2(buf[span, :] * exp2_scale - shift)
        buf[span, :] = tile
        return mass + jnp.where(k < count, jnp.sum(rows_of(tile), axis=0), 0.0)

    def add_part(buf, k, share):
        span = slice(k * BLK, (k + 1) * BLK)
        tile = buf[span, :] * share
        total[span, :] += tile[:, :BLK] + tile[:, BLK:]

    low = jnp.full((8, 2 * BLK), masked_value, F32)
    parts = KEYS // chunk
    step_slots = SEL // (parts // 2)

    def both(p, buf, done, shift):
        peak = low
        if p is not None:
            pair = jnp.concatenate([qa[p], qb[p]], axis=1)
        mass = jnp.zeros((8, 2 * BLK), F32)
        for k in range(parts // 2):
            if p is not None:
                peak = score_part(pair, buf, k, peak)
            if done is not None:
                for n in range(step_slots * k, step_slots * (k + 1)):
                    mass = exp_part(done, n, shift, mass)
        if done is not None:
            share = 1.0 / (jnp.sum(mass, axis=0, keepdims=True) * H)
        for k in range(parts // 2):
            if p is not None:
                peak = score_part(pair, buf, parts // 2 + k, peak)
            if done is not None:
                for n in range(step_slots * k, step_slots * (k + 1)):
                    add_part(done, n, share)
        return jnp.max(peak, axis=0, keepdims=True) * exp2_scale

    def step(k, shift):
        shift = both(2 * k + 1, buf_b, buf_a, shift)
        return both(2 * k + 2, buf_a, buf_b, shift)

    pairs = qa.shape[0]
    shift = both(0, buf_a, None, None)
    shift = lax.fori_loop(0, pairs // 2 - 1, step, shift)
    shift = both(pairs - 1, buf_b, buf_a, shift)
    both(None, None, buf_b, shift)
    tail = tail_tile(split_rows(stats[0:1, :]) + split_rows(stats[1:2, :]))
    for s, out in enumerate((o0, o1, o2, o3)):
        start = pl.multiple_of(lax.rem(y + s, NY) * OWNK, OWNK)
        used = lax.broadcasted_iota(I32, (OWNK, BLK), 0) + start < count * BLK
        out[:OWNK, :] = jnp.where(used, total[pl.ds(start, OWNK), :], 0.0).astype(BF16)
        out[OWNK:, :] = tail


def loss_kernel(t0, t1, t2, t3, logits, out):
    pieces = (t0, t1, t2, t3)
    tails = [t[OWNK:, :].astype(F32) for t in pieces]
    peaks = [t[0:1] + t[1:2] + t[2:3] for t in tails]
    masses = [t[3:4] + t[4:5] + t[5:6] for t in tails]
    peak = functools.reduce(jnp.maximum, peaks)
    mass = functools.reduce(jnp.add, [m * jnp.exp(p - peak) for m, p in zip(masses, peaks)])
    log_total = peak + jnp.log(mass)
    target = functools.reduce(jnp.add, [t[:OWNK, :].astype(F32) for t in pieces])
    masked = logits[...]
    valid = masked > 0.5 * masked_value
    log_probs = masked - log_total
    entropy = -jnp.sum(jnp.where(valid, target * log_probs, 0.0), axis=0, keepdims=True)
    grad = jnp.where(valid, jnp.exp(log_probs) - target, 0.0) / QUERIES
    out[:OWNK, :] = grad.astype(BF16)
    out[OWNK:, :] = tail_tile(split_rows(entropy))


def backward_kernel(
    g0, g1, g2, g3, i0, i1, i2, i3, iq, out, entropy_ref, keys, keys_t, grads
):
    y = lax.axis_index("y")
    entropy = jnp.zeros((1, BLK), F32)
    for s, piece in enumerate((g0, g1, g2, g3)):
        start = pl.multiple_of(lax.rem(y + NY - s, NY) * OWNK, OWNK)
        grads[pl.ds(start, OWNK), :] = piece[:OWNK, :].astype(F32)
        tail = piece[OWNK:, :].astype(F32)
        entropy = entropy + tail[0:1] + tail[1:2] + tail[2:3]
    entropy_ref[...] = jnp.broadcast_to(entropy, (8, BLK))
    for s, piece in enumerate((i0, i1, i2, i3)):
        start = pl.multiple_of(lax.rem(y + NY - s, NY) * IDXC, IDXC)
        for j in range(SEL):
            keys[pl.ds(start, IDXC), j * BLK : (j + 1) * BLK] = piece[j]
    for j in range(SEL):
        keys_t[j * BLK : (j + 1) * BLK, :] = keys[:, j * BLK : (j + 1) * BLK].T
    chunk = 512
    for core in range(2):
        ref = iq.at[core]
        rows = head_rows(ref[HALF_COLS:, :])
        for p in range(4):
            a, b = 2 * p, 2 * p + 1
            pair = jnp.concatenate(
                [ref[a * ID : (a + 1) * ID, :], ref[b * ID : (b + 1) * ID, :]], axis=1
            )
            acc = jnp.zeros((ID, 2 * BLK), F32)
            for k in range(KEYS // chunk):
                span = slice(k * chunk, (k + 1) * chunk)
                affinity = jnp.dot(keys_t[span, :], pair, preferred_element_type=F32)
                grad = grads[span, :]
                scaled = jnp.concatenate([grad * rows[a : a + 1], grad * rows[b : b + 1]], axis=1)
                masked = jnp.where(affinity > 0, scaled, 0.0).astype(BF16)
                acc = acc + jnp.dot(keys[:, span], masked, preferred_element_type=F32)
            acc = acc.astype(BF16)
            for n, head in enumerate((a, b)):
                lanes = slice(n * BLK, (n + 1) * BLK)
                out[2 * owner_of_piece(2 * head) + core] = acc[:COLS, lanes]
                out[2 * owner_of_piece(2 * head + 1) + core] = acc[COLS:, lanes]


def owner_of_piece(piece):
    k, x = piece // 4, piece % 4
    return (k - 2 * x) % 4 * 4 + x


def weight_kernel(qg, xa, xb, out, lhs, own_x, sems):
    parts = sems.shape[0]
    span = QUERIES // parts
    copies = []
    for k in range(parts):
        rows = pl.ds(k * span, span)
        copies.append(pltpu.make_async_copy(xa.at[rows, :], own_x.at[rows, :], sems.at[k]))
        copies[-1].start()
    for s in range(2 * NQ):
        lhs[:, s * BLK : (s + 1) * BLK] = qg[s]
    other = jnp.dot(lhs[...], xb[...], preferred_element_type=F32).astype(BF16)
    own = jnp.zeros(other.shape, F32)
    for k in range(parts):
        rows = slice(k * span, (k + 1) * span)
        copies[k].wait()
        own = own + jnp.dot(lhs[:, rows], own_x[rows, :], preferred_element_type=F32)
    own = own.astype(BF16)
    own_first = jnp.broadcast_to(lax.axis_index("c") == 0, own.shape)
    half = own.shape[1]
    out[:, :half] = jnp.where(own_first, own, other)
    out[:, half:] = jnp.where(own_first, other, own)


def quarter_kernel(p0, p1, p2, p3, full, top, bottom, rows):
    x = lax.axis_index("x")
    for s, piece in enumerate((p0, p1, p2, p3)):
        start = pl.multiple_of(lax.rem(x + 4 - s, 4) * COLS, COLS)
        rows[pl.ds(start, COLS), :] = piece[...]
    for k in range(6):
        tile = rows[:, k * 256 : (k + 1) * 256].T
        full[k * 256 : (k + 1) * 256, :] = tile
        half = top if k < 3 else bottom
        half[k % 3 * 256 : (k % 3 + 1) * 256, :] = tile


def finish_kernel(own, below, above, top, bottom, out, wide, sems):
    colour = lax.rem(lax.axis_index("z") + 2 * lax.axis_index("x"), 4)
    half = DQ // 2
    copies = []
    for n, (shift, pieces) in enumerate(
        ((0, (own,)), (2, (top, bottom)), (3, (below,)), (1, (above,)))
    ):
        for m, piece in enumerate(pieces):
            wide[n, m * half : m * half + piece.shape[0], :] = piece[...].astype(F32)
        lanes = pl.multiple_of(lax.rem(colour + shift, 4) * 256, 256)
        copies.append(pltpu.make_async_copy(wide.at[n], out.at[:, pl.ds(lanes, 256)], sems.at[n]))
        copies[-1].start()
    for c in copies:
        c.wait()


def plane(dz, dx):
    return [
        (z * 4 + x, (z + dz) % 4 * 4 + (x + dx) % 4) for z in range(4) for x in range(4)
    ]


def ring(shift):
    return [(i, (i + shift) % NY) for i in range(NY)]


SWAP = [(0, 1), (1, 0)]
SHIFTS = (1, 3, 2)


def around_y(array):
    moved = {s: lax.ppermute(array, "y", ring(s)) for s in SHIFTS}
    return (array, moved[1], moved[2], moved[3])


def on_device(
    q_absorbed, key_cache, index_input, index_weight, head_weights, block_ids, block_counts
):
    y, core, _ = place()
    ids = block_ids.T

    outgoing = call(
        pick_outgoing_kernel,
        shape((NQ, CAP, PIECE, BLK), BF16),
        [SMEM, ANY],
        VMEM,
        [pltpu.SemaphoreType.DMA((2,))],
        "pick_outgoing",
    )(ids, in_hbm(key_cache))
    arrived = lax.all_to_all(outgoing, ("z", "x"), split_axis=0, concat_axis=0, tiled=True)

    iq_own, iq_send = call(
        index_query_kernel,
        (shape((IQ_ROWS, BLK), BF16),) * 2,
        [VMEM, VMEM, VMEM],
        (VMEM, VMEM),
        name="index_query",
    )(index_input, index_weight, head_weights.T)
    iq_other = lax.ppermute(iq_send, "c", SWAP)
    first = core == 0
    iq_pair = jnp.stack(
        [jnp.where(first, iq_own, iq_other), jnp.where(first, iq_other, iq_own)]
    )
    iq_all = around_y(iq_pair)

    q_t = jnp.transpose(q_absorbed, (1, 2, 0))
    q_send = lax.dynamic_slice_in_dim(q_t, (1 - core) * BLK, BLK, 2)
    q_other = lax.ppermute(q_send, "c", SWAP)

    lat, idx = call(
        pick_listed_kernel,
        (shape((SEL, LATC, BLK), BF16), shape((SEL, IDXC, BLK), BF16)),
        [SMEM] + [ANY] * 5,
        (VMEM, VMEM),
        [pltpu.SMEM((NQ,), I32), pltpu.SemaphoreType.DMA((2,))],
        "pick_listed",
    )(ids, arrived, q_send, *iq_all[1:])
    idx_all = around_y(idx)
    lat_sent = lax.optimization_barrier((lat, *idx_all[1:]))[0]
    lat_all = (lat, *around_y(lat_sent)[1:])

    half = DQ // 2
    x_half = lax.dynamic_slice_in_dim(index_input, core * half, half, 1)
    x_half, _ = lax.optimization_barrier((x_half, idx))
    x_own = lax.all_gather(x_half, ("z", "x"), axis=0, tiled=True)

    logits, stats = call(
        logits_kernel,
        (shape((OWNK, BLK), F32), shape((8, BLK), F32)),
        [SMEM] + [VMEM] * 8,
        (VMEM, VMEM),
        [pltpu.VMEM((ID, OWNK), BF16), pltpu.VMEM((OWNK, BLK), F32)],
        "index_logits",
    )(block_counts, *map(in_vmem, (*idx_all, *iq_all)))

    targets = call(
        target_kernel,
        (shape((LG_ROWS, BLK), BF16),) * 4,
        [SMEM, VMEM] + [VMEM] * 4 + [ANY, VMEM],
        (VMEM,) * 4,
        [
            pltpu.VMEM((DK, KEYS), BF16),
            pltpu.VMEM((KEYS, DK), BF16),
            pltpu.VMEM((16, DK, BLK), BF16),
            pltpu.VMEM((KEYS, 2 * BLK), F32),
            pltpu.VMEM((KEYS, 2 * BLK), F32),
            pltpu.VMEM((KEYS, BLK), F32),
            pltpu.SemaphoreType.DMA((2,)),
        ],
        "attention_target",
    )(block_counts, stats, *map(in_vmem, lat_all), in_hbm(q_t), in_vmem(q_other))
    x_own, _ = lax.optimization_barrier((x_own, targets[0]))
    x_other = lax.ppermute(x_own, "c", SWAP)
    arrived_targets = {s: lax.ppermute(targets[s], "y", ring(s)) for s in SHIFTS}

    grads = call(
        loss_kernel,
        shape((LG_ROWS, BLK), BF16),
        [VMEM] * 5,
        VMEM,
        name="loss",
    )(*map(in_vmem, (targets[0], *(arrived_targets[s] for s in (1, 2, 3)), logits)))
    grads_all = around_y(grads)

    query_grad, entropy = call(
        backward_kernel,
        (shape((2 * NQ, COLS, BLK), BF16), shape((8, BLK), F32)),
        [VMEM] * 9,
        (VMEM, VMEM),
        [
            pltpu.VMEM((ID, KEYS), BF16),
            pltpu.VMEM((KEYS, ID), BF16),
            pltpu.VMEM((KEYS, BLK), F32),
        ],
        "index_backward",
    )(*map(in_vmem, (*grads_all, *idx_all, iq_pair)))
    entropy_other = lax.ppermute(entropy, "c", SWAP)
    entropy_both = jnp.where(
        first,
        jnp.concatenate([entropy[0], entropy_other[0]]),
        jnp.concatenate([entropy_other[0], entropy[0]]),
    )
    share = 2 * BLK // (2 * NY)
    entropy_mine = lax.dynamic_slice_in_dim(entropy_both, (2 * y + core) * share, share, 0)

    swapped = lax.all_to_all(query_grad, ("z", "x", "c"), split_axis=0, concat_axis=0, tiled=True)
    qblk = ("z", "x")
    piece = call(
        weight_kernel,
        shape((COLS, DQ), BF16),
        [VMEM, ANY, VMEM],
        VMEM,
        [
            pltpu.VMEM((COLS, QUERIES), BF16),
            pltpu.VMEM((QUERIES, half), BF16),
            pltpu.SemaphoreType.DMA((4,)),
        ],
        "weight_piece",
    )(in_vmem(swapped), in_hbm(x_own), in_vmem(x_other))
    same = [piece] + [lax.ppermute(piece, qblk, plane(-2 * d, d)) for d in (1, 2, 3)]
    full, top, bottom = call(
        quarter_kernel,
        (shape((DQ, 256), BF16), shape((half, 256), BF16), shape((half, 256), BF16)),
        [VMEM] * 4,
        (VMEM,) * 3,
        [pltpu.VMEM((256, DQ), BF16)],
        "quarter",
    )(*map(in_vmem, same))
    below = lax.ppermute(full, qblk, plane(1, 0))
    above = lax.ppermute(full, qblk, plane(-1, 0))
    top = lax.ppermute(top, qblk, plane(0, -1))
    bottom = lax.ppermute(bottom, qblk, plane(0, 1))
    weight_grad = call(
        finish_kernel,
        shape((DQ, HALF_COLS), F32),
        [VMEM] * 5,
        ANY,
        [pltpu.VMEM((4, DQ, 256), F32), pltpu.SemaphoreType.DMA((4,))],
        "finish",
    )(*map(in_vmem, (full, below, above, top, bottom)))
    return weight_grad, entropy_mine


def solution(mesh):
    fine = Mesh(mesh.devices.reshape(NY, 2, 4, 4), ("y", "c", "z", "x"))
    head, qblk = ("y", "c"), ("z", "x")
    placed = (
        P(qblk, head, None),
        P(qblk, None, None),
        P(qblk, None),
        P(None, head),
        P(qblk, head),
        P(),
        P(),
    )
    return jax.shard_map(
        on_device,
        mesh=fine,
        in_specs=placed,
        out_specs=(P(None, head), P(qblk + head)),
        check_vma=False,
    )
```

```python
import functools

import jax
import jax.numpy as jnp
from jax import lax
from jax.experimental import pallas as pl
from jax.experimental.pallas import tpu as pltpu
from jax.sharding import Mesh, PartitionSpec as P

BF16 = jnp.bfloat16
F32 = jnp.float32
I32 = jnp.int32

H = 128
DK = 576
ID = 128
CAP = 3
BLK = 128
SEL = 16
KEYS = SEL * BLK
NY = 4
NQ = 16
SHARD = 32
LATC = DK // NY
IDXC = ID // NY
PIECE = LATC + IDXC
OWNK = KEYS // NY
HALF_COLS = 1024
IQ_ROWS = HALF_COLS + 32
LG_ROWS = OWNK + 16
DQ = 1536
COLS = HALF_COLS // NQ
QUERIES = 4096

score_scale = 192.0 ** (-0.5)
exp2_scale = score_scale * 1.4426950408889634
masked_value = -1e30
VMEM_LIMIT = 24 * 1024 * 1024

ANY = pl.BlockSpec(memory_space=pl.ANY)
VMEM = pl.BlockSpec(memory_space=pltpu.VMEM)
SMEM = pl.BlockSpec(memory_space=pltpu.SMEM)
HBM = pl.BlockSpec(memory_space=pltpu.HBM)


def call(kernel, out_shape, in_specs, out_specs, scratch=(), name=None):
    return pl.pallas_call(
        kernel,
        out_shape=out_shape,
        in_specs=in_specs,
        out_specs=out_specs,
        scratch_shapes=list(scratch),
        compiler_params=pltpu.CompilerParams(vmem_limit_bytes=VMEM_LIMIT),
        name=name,
    )


def shape(dims, dtype):
    return jax.ShapeDtypeStruct(dims, dtype)


def in_hbm(array):
    return pltpu.with_memory_space_constraint(array, pltpu.HBM)


def in_vmem(array):
    return pltpu.with_memory_space_constraint(array, pltpu.VMEM)


def place():
    return lax.axis_index("y"), lax.axis_index("c"), lax.axis_index(("z", "x"))


def slots_in_use(counts):
    _, core, me = place()
    return counts[2 * me + core]


def pick_outgoing_kernel(ids, cache, out, found, sem):
    y, core, me = place()
    rows = pl.ds(pl.multiple_of(y * PIECE, 16), PIECE)
    first = me * SHARD

    def copy(block, place_out):
        return pltpu.make_async_copy(cache.at[block, rows, :], out.at[place_out], sem)

    def per_dst(dst, total):
        count = jnp.int32(0)
        for s in range(SEL):
            local = ids[s, 2 * dst + core] - first
            found[total + count] = local * (NQ * CAP) + dst * CAP + jnp.minimum(count, CAP - 1)
            count = count + ((local >= 0) & (local < SHARD)).astype(I32)
        return total + count

    total = lax.fori_loop(0, NQ, per_dst, jnp.int32(0))

    def start(n, carry):
        code = found[n]
        block = code // (NQ * CAP)
        copy(block, code - block * (NQ * CAP)).start()
        return carry

    def wait(n, carry):
        copy(0, 0).wait()
        return carry

    lax.fori_loop(0, total, start, 0)
    lax.fori_loop(0, total, wait, 0)


def pick_listed_kernel(ids, arrived, *refs):
    sent, listed, seen, sem = refs[-4:]
    _, core, me = place()
    row = 2 * me + core
    for i in range(NQ):
        seen[i] = 0
    pending = []
    for s in range(SEL):
        owner = lax.shift_right_logical(ids[s, row], 5)
        rank = jnp.minimum(seen[owner], CAP - 1)
        seen[owner] = seen[owner] + 1
        pending.append(pltpu.make_async_copy(arrived.at[owner * CAP + rank], listed.at[s], sem.at[0]))
        pending[-1].start()
    for c in pending:
        c.wait()
    out = pltpu.make_async_copy(listed, sent, sem.at[1])
    out.start()
    out.wait()


def index_query_kernel(x, w, hw, mine, other):
    core = lax.axis_index("c")
    for k in range(4):
        cols = HALF_COLS // 4
        part = jnp.dot(x[...], w[:, k * cols : (k + 1) * cols], preferred_element_type=F32)
        part = part.astype(BF16)
        low = part[:BLK].T
        high = part[BLK:].T
        rows = pl.ds(k * cols, cols)
        first = jnp.broadcast_to(core == 0, low.shape)
        mine[rows, :] = jnp.where(first, low, high)
        other[rows, :] = jnp.where(first, high, low)
    weights = hw[...]
    hi = weights.astype(BF16)
    rest = weights - hi.astype(F32)
    mid = rest.astype(BF16)
    lo = (rest - mid.astype(F32)).astype(BF16)
    ext = jnp.concatenate(
        [hi.astype(F32), mid.astype(F32), lo.astype(F32), jnp.zeros_like(weights)], axis=0
    )
    first = jnp.broadcast_to(core == 0, (32, BLK))
    tail = pl.ds(HALF_COLS, 32)
    mine[tail, :] = jnp.where(first, ext[:, :BLK], ext[:, BLK:]).astype(BF16)
    other[tail, :] = jnp.where(first, ext[:, BLK:], ext[:, :BLK]).astype(BF16)


def head_rows(tail):
    tail = tail.astype(F32)
    return tail[0:8] + tail[8:16] + tail[16:24]


def logits_kernel(counts, p0, p1, p2, p3, iq0, iq1, iq2, iq3, *rest):
    logits_ref, stats_ref, latent_t, keys_out, keys_t_out, index_t, keys, total, own, sems = rest
    y, count = lax.axis_index("y"), slots_in_use(counts)
    load = pltpu.make_async_copy(p0, own, sems.at[2])
    load.start()
    for s, piece in ((1, p1), (2, p2), (3, p3), (0, own)):
        if s == 0:
            load.wait()
        rows = pl.ds(pl.multiple_of(lax.rem(y + NY - s, NY) * PIECE, 16), PIECE)
        for j in range(SEL):
            keys[rows, j * BLK : (j + 1) * BLK] = piece[j]
    copies = [pltpu.make_async_copy(keys.at[pl.ds(DK, ID), :], keys_out, sems.at[0])]
    copies[0].start()
    for j in range(SEL):
        span = slice(j * BLK, (j + 1) * BLK)
        latent_t[span, :] = keys[:DK, span].T
        index_t[span, :] = keys[DK:, span].T
    copies.append(pltpu.make_async_copy(index_t, keys_t_out, sems.at[1]))
    copies[1].start()
    iq_refs = (iq0, iq1, iq2, iq3)
    keys_t = index_t[pl.ds(pl.multiple_of(y * OWNK, OWNK), OWNK), :]
    total[...] = jnp.zeros_like(total)
    for ref in [r.at[n] for r in iq_refs for n in range(2)]:
        rows = head_rows(ref[HALF_COLS:, :])
        for p in range(4):
            a, b = 2 * p, 2 * p + 1
            pair = jnp.concatenate(
                [ref[a * ID : (a + 1) * ID, :], ref[b * ID : (b + 1) * ID, :]], axis=1
            )
            affinity = jnp.maximum(jnp.dot(keys_t, pair, preferred_element_type=F32), 0.0)
            total[...] += (
                affinity[:, :BLK] * rows[a : a + 1] + affinity[:, BLK:] * rows[b : b + 1]
            )
    key = lax.broadcasted_iota(I32, (OWNK, BLK), 0) + y * OWNK
    token = lax.broadcasted_iota(I32, (OWNK, BLK), 1)
    valid = (key < count * BLK) & ((key >= BLK) | (key <= token))
    masked = jnp.where(valid, total[...], masked_value)
    logits_ref[...] = masked
    peak = jnp.max(masked, axis=0, keepdims=True)
    mass = jnp.sum(jnp.exp(masked - peak), axis=0, keepdims=True)
    row = lax.broadcasted_iota(I32, (8, BLK), 0)
    stats_ref[...] = jnp.where(row == 0, peak, mass)
    for c in copies:
        c.wait()


def split_rows(row):
    hi = row.astype(BF16).astype(F32)
    mid = (row - hi).astype(BF16).astype(F32)
    return hi, mid, row - hi - mid


def tail_tile(rows):
    at = lax.broadcasted_iota(I32, (16, BLK), 0)
    tile = jnp.zeros((16, BLK), F32)
    for n, row in enumerate(rows):
        tile = jnp.where(at == n, row, tile)
    return tile.astype(BF16)


def target_kernel(
    counts, stats, keys_t, q_own, qb, o0, o1, o2, o3, qa, buf_a, buf_b, total, sem
):
    y, core, _ = place()
    count = slots_in_use(counts)
    lanes = pl.multiple_of(core * BLK, BLK)
    own = pltpu.make_async_copy(q_own.at[:, :, pl.ds(lanes, BLK)], qa, sem)
    own.start()
    total[...] = jnp.zeros_like(total)
    own.wait()

    chunk = 1024
    token = lax.broadcasted_iota(I32, (BLK, 2 * BLK), 1) % BLK
    causal = lax.broadcasted_iota(I32, (BLK, 2 * BLK), 0) <= token

    def rows_of(tile):
        return tile.reshape(tile.shape[0] // 8, 8, 2 * BLK)

    def score_part(pair, buf, k, peak):
        part = jnp.dot(keys_t[k * chunk : (k + 1) * chunk, :], pair, preferred_element_type=F32)
        for j in range(chunk // BLK):
            slot = k * (chunk // BLK) + j
            tile = part[j * BLK : (j + 1) * BLK]
            if slot == 0:
                tile = jnp.where(causal, tile, masked_value)
            buf[slot * BLK : (slot + 1) * BLK, :] = tile
            top = jnp.max(rows_of(tile), axis=0)
            peak = jnp.maximum(peak, jnp.where(slot < count, top, masked_value))
        return peak

    def exp_part(buf, k, shift, mass):
        span = slice(k * BLK, (k + 1) * BLK)
        tile = jnp.exp2(buf[span, :] * exp2_scale - shift)
        buf[span, :] = tile
        return mass + jnp.where(k < count, jnp.sum(rows_of(tile), axis=0), 0.0)

    def add_part(buf, k, share):
        span = slice(k * BLK, (k + 1) * BLK)
        tile = buf[span, :] * share
        total[span, :] += tile[:, :BLK] + tile[:, BLK:]

    low = jnp.full((8, 2 * BLK), masked_value, F32)
    parts = KEYS // chunk
    step_slots = SEL // (parts // 2)

    def both(p, buf, done, shift):
        peak = low
        if p is not None:
            pair = jnp.concatenate([qa[p], qb[p]], axis=1)
        mass = jnp.zeros((8, 2 * BLK), F32)
        for k in range(parts // 2):
            if p is not None:
                peak = score_part(pair, buf, k, peak)
            if done is not None:
                for n in range(step_slots * k, step_slots * (k + 1)):
                    mass = exp_part(done, n, shift, mass)
        if done is not None:
            share = 1.0 / (jnp.sum(mass, axis=0, keepdims=True) * H)
        for k in range(parts // 2):
            if p is not None:
                peak = score_part(pair, buf, parts // 2 + k, peak)
            if done is not None:
                for n in range(step_slots * k, step_slots * (k + 1)):
                    add_part(done, n, share)
        return jnp.max(peak, axis=0, keepdims=True) * exp2_scale

    def step(k, shift):
        shift = both(2 * k + 1, buf_b, buf_a, shift)
        return both(2 * k + 2, buf_a, buf_b, shift)

    pairs = qa.shape[0]
    shift = both(0, buf_a, None, None)
    shift = lax.fori_loop(0, pairs // 2 - 1, step, shift)
    shift = both(pairs - 1, buf_b, buf_a, shift)
    both(None, None, buf_b, shift)
    tail = tail_tile(split_rows(stats[0:1, :]) + split_rows(stats[1:2, :]))
    for s, out in enumerate((o0, o1, o2, o3)):
        start = pl.multiple_of(lax.rem(y + s, NY) * OWNK, OWNK)
        used = lax.broadcasted_iota(I32, (OWNK, BLK), 0) + start < count * BLK
        out[:OWNK, :] = jnp.where(used, total[pl.ds(start, OWNK), :], 0.0).astype(BF16)
        out[OWNK:, :] = tail


def loss_kernel(t0, t1, t2, t3, logits, out):
    pieces = (t0, t1, t2, t3)
    tails = [t[OWNK:, :].astype(F32) for t in pieces]
    peaks = [t[0:1] + t[1:2] + t[2:3] for t in tails]
    masses = [t[3:4] + t[4:5] + t[5:6] for t in tails]
    peak = functools.reduce(jnp.maximum, peaks)
    mass = functools.reduce(jnp.add, [m * jnp.exp(p - peak) for m, p in zip(masses, peaks)])
    log_total = peak + jnp.log(mass)
    target = functools.reduce(jnp.add, [t[:OWNK, :].astype(F32) for t in pieces])
    masked = logits[...]
    valid = masked > 0.5 * masked_value
    log_probs = masked - log_total
    entropy = -jnp.sum(jnp.where(valid, target * log_probs, 0.0), axis=0, keepdims=True)
    grad = jnp.where(valid, jnp.exp(log_probs) - target, 0.0) / QUERIES
    out[:OWNK, :] = grad.astype(BF16)
    out[OWNK:, :] = tail_tile(split_rows(entropy))


def backward_kernel(g0, g1, g2, g3, keys, keys_t, iq, out, entropy_ref, grads):
    y = lax.axis_index("y")
    entropy = jnp.zeros((1, BLK), F32)
    for s, piece in enumerate((g0, g1, g2, g3)):
        start = pl.multiple_of(lax.rem(y + NY - s, NY) * OWNK, OWNK)
        grads[pl.ds(start, OWNK), :] = piece[:OWNK, :].astype(F32)
        tail = piece[OWNK:, :].astype(F32)
        entropy = entropy + tail[0:1] + tail[1:2] + tail[2:3]
    entropy_ref[...] = jnp.broadcast_to(entropy, (8, BLK))
    chunk = 512
    for core in range(2):
        ref = iq.at[core]
        rows = head_rows(ref[HALF_COLS:, :])
        for p in range(4):
            a, b = 2 * p, 2 * p + 1
            pair = jnp.concatenate(
                [ref[a * ID : (a + 1) * ID, :], ref[b * ID : (b + 1) * ID, :]], axis=1
            )
            acc = jnp.zeros((ID, 2 * BLK), F32)
            for k in range(KEYS // chunk):
                span = slice(k * chunk, (k + 1) * chunk)
                affinity = jnp.dot(keys_t[span, :], pair, preferred_element_type=F32)
                grad = grads[span, :]
                scaled = jnp.concatenate([grad * rows[a : a + 1], grad * rows[b : b + 1]], axis=1)
                masked = jnp.where(affinity > 0, scaled, 0.0).astype(BF16)
                acc = acc + jnp.dot(keys[:, span], masked, preferred_element_type=F32)
            acc = acc.astype(BF16)
            for n, head in enumerate((a, b)):
                lanes = slice(n * BLK, (n + 1) * BLK)
                out[2 * owner_of_piece(2 * head) + core] = acc[:COLS, lanes]
                out[2 * owner_of_piece(2 * head + 1) + core] = acc[COLS:, lanes]


def owner_of_piece(piece):
    k, x = piece // 4, piece % 4
    return (k - 2 * x) % 4 * 4 + x


def weight_kernel(qg, xa, xb, out, lhs, own_x, sems):
    parts = sems.shape[0]
    span = QUERIES // parts
    copies = []
    for k in range(parts):
        rows = pl.ds(k * span, span)
        copies.append(pltpu.make_async_copy(xa.at[rows, :], own_x.at[rows, :], sems.at[k]))
        copies[-1].start()
    for s in range(2 * NQ):
        lhs[:, s * BLK : (s + 1) * BLK] = qg[s]
    other = jnp.dot(lhs[...], xb[...], preferred_element_type=F32).astype(BF16)
    own = jnp.zeros(other.shape, F32)
    for k in range(parts):
        rows = slice(k * span, (k + 1) * span)
        copies[k].wait()
        own = own + jnp.dot(lhs[:, rows], own_x[rows, :], preferred_element_type=F32)
    own = own.astype(BF16)
    own_first = jnp.broadcast_to(lax.axis_index("c") == 0, own.shape)
    half = own.shape[1]
    out[:, :half] = jnp.where(own_first, own, other)
    out[:, half:] = jnp.where(own_first, other, own)


def quarter_kernel(p0, p1, p2, p3, full, top, bottom, rows):
    x = lax.axis_index("x")
    for s, piece in enumerate((p0, p1, p2, p3)):
        start = pl.multiple_of(lax.rem(x + 4 - s, 4) * COLS, COLS)
        rows[pl.ds(start, COLS), :] = piece[...]
    for k in range(6):
        tile = rows[:, k * 256 : (k + 1) * 256].T
        full[k * 256 : (k + 1) * 256, :] = tile
        half = top if k < 3 else bottom
        half[k % 3 * 256 : (k % 3 + 1) * 256, :] = tile


def finish_kernel(own, below, above, top, bottom, out, wide, sems):
    colour = lax.rem(lax.axis_index("z") + 2 * lax.axis_index("x"), 4)
    half = DQ // 2
    copies = []
    for n, (shift, pieces) in enumerate(
        ((0, (own,)), (2, (top, bottom)), (3, (below,)), (1, (above,)))
    ):
        for m, piece in enumerate(pieces):
            wide[n, m * half : m * half + piece.shape[0], :] = piece[...].astype(F32)
        lanes = pl.multiple_of(lax.rem(colour + shift, 4) * 256, 256)
        copies.append(pltpu.make_async_copy(wide.at[n], out.at[:, pl.ds(lanes, 256)], sems.at[n]))
        copies[-1].start()
    for c in copies:
        c.wait()


def plane(dz, dx):
    return [
        (z * 4 + x, (z + dz) % 4 * 4 + (x + dx) % 4) for z in range(4) for x in range(4)
    ]


def ring(shift):
    return [(i, (i + shift) % NY) for i in range(NY)]


SWAP = [(0, 1), (1, 0)]
SHIFTS = (1, 3, 2)


def around_y(array):
    moved = {s: lax.ppermute(array, "y", ring(s)) for s in SHIFTS}
    return (array, moved[1], moved[2], moved[3])


def on_device(
    q_absorbed, key_cache, index_input, index_weight, head_weights, block_ids, block_counts
):
    y, core, _ = place()
    ids = block_ids.T

    outgoing = call(
        pick_outgoing_kernel,
        shape((NQ * CAP, PIECE, BLK), BF16),
        [SMEM, ANY],
        VMEM,
        [pltpu.SMEM((NQ * SEL + 1,), I32), pltpu.SemaphoreType.DMA],
        "pick_outgoing",
    )(ids, in_hbm(key_cache))
    arrived = lax.all_to_all(outgoing, ("z", "x"), split_axis=0, concat_axis=0, tiled=True)

    iq_own, iq_send = call(
        index_query_kernel,
        (shape((IQ_ROWS, BLK), BF16),) * 2,
        [VMEM, VMEM, VMEM],
        (VMEM, VMEM),
        name="index_query",
    )(index_input, index_weight, head_weights.T)
    iq_other = lax.ppermute(iq_send, "c", SWAP)
    first = core == 0
    iq_pair = jnp.stack(
        [jnp.where(first, iq_own, iq_other), jnp.where(first, iq_other, iq_own)]
    )
    iq_all = around_y(iq_pair)

    q_t = jnp.transpose(q_absorbed, (1, 2, 0))
    q_send = lax.dynamic_slice_in_dim(q_t, (1 - core) * BLK, BLK, 2)
    q_other = lax.ppermute(q_send, "c", SWAP)

    listed = call(
        pick_listed_kernel,
        pltpu.HBM((SEL, PIECE, BLK), BF16),
        [SMEM] + [ANY] * 5,
        HBM,
        [
            pltpu.VMEM((SEL, PIECE, BLK), BF16),
            pltpu.SMEM((NQ,), I32),
            pltpu.SemaphoreType.DMA((2,)),
        ],
        "pick_listed",
    )(ids, arrived, q_send, *iq_all[1:])
    pieces = around_y(listed)

    half = DQ // 2
    x_half = lax.dynamic_slice_in_dim(index_input, core * half, half, 1)
    x_half, _ = lax.optimization_barrier((x_half, listed))
    x_own = lax.all_gather(x_half, ("z", "x"), axis=0, tiled=True)

    logits, stats, latent_t, index_keys, index_t = call(
        logits_kernel,
        (
            shape((OWNK, BLK), F32),
            shape((8, BLK), F32),
            shape((KEYS, DK), BF16),
            pltpu.HBM((ID, KEYS), BF16),
            pltpu.HBM((KEYS, ID), BF16),
        ),
        [SMEM, ANY] + [VMEM] * 7,
        (VMEM, VMEM, VMEM, HBM, HBM),
        [
            pltpu.VMEM((KEYS, ID), BF16),
            pltpu.VMEM((DK + ID, KEYS), BF16),
            pltpu.VMEM((OWNK, BLK), F32),
            pltpu.VMEM((SEL, PIECE, BLK), BF16),
            pltpu.SemaphoreType.DMA((3,)),
        ],
        "index_logits",
    )(block_counts, in_hbm(pieces[0]), *map(in_vmem, (*pieces[1:], *iq_all)))

    targets = call(
        target_kernel,
        (shape((LG_ROWS, BLK), BF16),) * 4,
        [SMEM, VMEM, VMEM, ANY, VMEM],
        (VMEM,) * 4,
        [
            pltpu.VMEM((16, DK, BLK), BF16),
            pltpu.VMEM((KEYS, 2 * BLK), F32),
            pltpu.VMEM((KEYS, 2 * BLK), F32),
            pltpu.VMEM((KEYS, BLK), F32),
            pltpu.SemaphoreType.DMA,
        ],
        "attention_target",
    )(block_counts, stats, in_vmem(latent_t), in_hbm(q_t), in_vmem(q_other))
    x_own, _ = lax.optimization_barrier((x_own, targets[0]))
    x_other = lax.ppermute(x_own, "c", SWAP)
    arrived_targets = {s: lax.ppermute(targets[s], "y", ring(s)) for s in SHIFTS}

    grads = call(
        loss_kernel,
        shape((LG_ROWS, BLK), BF16),
        [VMEM] * 5,
        VMEM,
        name="loss",
    )(*map(in_vmem, (targets[0], *(arrived_targets[s] for s in (1, 2, 3)), logits)))
    grads_all = around_y(grads)

    query_grad, entropy = call(
        backward_kernel,
        (shape((2 * NQ, COLS, BLK), BF16), shape((8, BLK), F32)),
        [VMEM] * 7,
        (VMEM, VMEM),
        [pltpu.VMEM((KEYS, BLK), F32)],
        "index_backward",
    )(*map(in_vmem, (*grads_all, index_keys, index_t, iq_pair)))
    entropy_other = lax.ppermute(entropy, "c", SWAP)
    entropy_both = jnp.where(
        first,
        jnp.concatenate([entropy[0], entropy_other[0]]),
        jnp.concatenate([entropy_other[0], entropy[0]]),
    )
    share = 2 * BLK // (2 * NY)
    entropy_mine = lax.dynamic_slice_in_dim(entropy_both, (2 * y + core) * share, share, 0)

    swapped = lax.all_to_all(query_grad, ("z", "x", "c"), split_axis=0, concat_axis=0, tiled=True)
    qblk = ("z", "x")
    piece = call(
        weight_kernel,
        shape((COLS, DQ), BF16),
        [VMEM, ANY, VMEM],
        VMEM,
        [
            pltpu.VMEM((COLS, QUERIES), BF16),
            pltpu.VMEM((QUERIES, half), BF16),
            pltpu.SemaphoreType.DMA((4,)),
        ],
        "weight_piece",
    )(in_vmem(swapped), in_hbm(x_own), in_vmem(x_other))
    same = [piece] + [lax.ppermute(piece, qblk, plane(-2 * d, d)) for d in (1, 2, 3)]
    full, top, bottom = call(
        quarter_kernel,
        (shape((DQ, 256), BF16), shape((half, 256), BF16), shape((half, 256), BF16)),
        [VMEM] * 4,
        (VMEM,) * 3,
        [pltpu.VMEM((256, DQ), BF16)],
        "quarter",
    )(*map(in_vmem, same))
    below = lax.ppermute(full, qblk, plane(1, 0))
    above = lax.ppermute(full, qblk, plane(-1, 0))
    top = lax.ppermute(top, qblk, plane(0, -1))
    bottom = lax.ppermute(bottom, qblk, plane(0, 1))
    weight_grad = call(
        finish_kernel,
        shape((DQ, HALF_COLS), F32),
        [VMEM] * 5,
        ANY,
        [pltpu.VMEM((4, DQ, 256), F32), pltpu.SemaphoreType.DMA((4,))],
        "finish",
    )(*map(in_vmem, (full, below, above, top, bottom)))
    return weight_grad, entropy_mine


def solution(mesh):
    fine = Mesh(mesh.devices.reshape(NY, 2, 4, 4), ("y", "c", "z", "x"))
    head, qblk = ("y", "c"), ("z", "x")
    placed = (
        P(qblk, head, None),
        P(qblk, None, None),
        P(qblk, None),
        P(None, head),
        P(qblk, head),
        P(),
        P(),
    )
    return jax.shard_map(
        on_device,
        mesh=fine,
        in_specs=placed,
        out_specs=(P(None, head), P(qblk + head)),
        check_vma=False,
    )
```

```python
import functools

import jax
import jax.numpy as jnp
from jax import lax
from jax.experimental import pallas as pl
from jax.experimental.pallas import tpu as pltpu
from jax.sharding import Mesh, PartitionSpec as P

BF16 = jnp.bfloat16
F32 = jnp.float32
I32 = jnp.int32

H = 128
DK = 576
ID = 128
CAP = 3
BLK = 128
SEL = 16
KEYS = SEL * BLK
NY = 4
NQ = 16
SHARD = 32
LATC = DK // NY
IDXC = ID // NY
PIECE = LATC + IDXC
OWNK = KEYS // NY
HALF_COLS = 1024
IQ_ROWS = HALF_COLS + 32
LG_ROWS = OWNK + 16
DQ = 1536
COLS = HALF_COLS // NQ
QUERIES = 4096

score_scale = 192.0 ** (-0.5)
exp2_scale = score_scale * 1.4426950408889634
masked_value = -1e30
VMEM_LIMIT = 24 * 1024 * 1024

ANY = pl.BlockSpec(memory_space=pl.ANY)
VMEM = pl.BlockSpec(memory_space=pltpu.VMEM)
SMEM = pl.BlockSpec(memory_space=pltpu.SMEM)
HBM = pl.BlockSpec(memory_space=pltpu.HBM)


def call(kernel, out_shape, in_specs, out_specs, scratch=(), name=None):
    return pl.pallas_call(
        kernel,
        out_shape=out_shape,
        in_specs=in_specs,
        out_specs=out_specs,
        scratch_shapes=list(scratch),
        compiler_params=pltpu.CompilerParams(vmem_limit_bytes=VMEM_LIMIT),
        name=name,
    )


def shape(dims, dtype):
    return jax.ShapeDtypeStruct(dims, dtype)


def in_hbm(array):
    return pltpu.with_memory_space_constraint(array, pltpu.HBM)


def in_vmem(array):
    return pltpu.with_memory_space_constraint(array, pltpu.VMEM)


def place():
    return lax.axis_index("y"), lax.axis_index("c"), lax.axis_index(("z", "x"))


def slots_in_use(counts):
    _, core, me = place()
    return counts[2 * me + core]


def pick_outgoing_kernel(ids, cache, out, found, sem):
    y, core, me = place()
    rows = pl.ds(pl.multiple_of(y * PIECE, 16), PIECE)
    first = me * SHARD

    def copy(block, place_out):
        return pltpu.make_async_copy(cache.at[block, rows, :], out.at[place_out], sem)

    def per_dst(dst, total):
        count = jnp.int32(0)
        for s in range(SEL):
            local = ids[s, 2 * dst + core] - first
            found[total + count] = local * (NQ * CAP) + dst * CAP + jnp.minimum(count, CAP - 1)
            count = count + ((local >= 0) & (local < SHARD)).astype(I32)
        return total + count

    total = lax.fori_loop(0, NQ, per_dst, jnp.int32(0))

    def start(n, carry):
        code = found[n]
        block = code // (NQ * CAP)
        copy(block, code - block * (NQ * CAP)).start()
        return carry

    def wait(n, carry):
        copy(0, 0).wait()
        return carry

    lax.fori_loop(0, total, start, 0)
    lax.fori_loop(0, total, wait, 0)


def pick_listed_kernel(ids, arrived, *refs):
    low, high, listed, seen, sem = refs[-5:]
    _, core, me = place()
    row = 2 * me + core
    for i in range(NQ):
        seen[i] = 0
    pending = []
    for s in range(SEL):
        owner = lax.shift_right_logical(ids[s, row], 5)
        rank = jnp.minimum(seen[owner], CAP - 1)
        seen[owner] = seen[owner] + 1
        pending.append(pltpu.make_async_copy(arrived.at[owner * CAP + rank], listed.at[s], sem.at[0]))
        pending[-1].start()
    for c in pending:
        c.wait()
    half = SEL // 2
    outs = [
        pltpu.make_async_copy(listed.at[pl.ds(n * half, half)], out, sem.at[1])
        for n, out in enumerate((low, high))
    ]
    for c in outs:
        c.start()
    for c in outs:
        c.wait()


def index_query_kernel(x, w, hw, mine, other):
    core = lax.axis_index("c")
    for k in range(4):
        cols = HALF_COLS // 4
        part = jnp.dot(x[...], w[:, k * cols : (k + 1) * cols], preferred_element_type=F32)
        part = part.astype(BF16)
        low = part[:BLK].T
        high = part[BLK:].T
        rows = pl.ds(k * cols, cols)
        first = jnp.broadcast_to(core == 0, low.shape)
        mine[rows, :] = jnp.where(first, low, high)
        other[rows, :] = jnp.where(first, high, low)
    weights = hw[...]
    hi = weights.astype(BF16)
    rest = weights - hi.astype(F32)
    mid = rest.astype(BF16)
    lo = (rest - mid.astype(F32)).astype(BF16)
    ext = jnp.concatenate(
        [hi.astype(F32), mid.astype(F32), lo.astype(F32), jnp.zeros_like(weights)], axis=0
    )
    first = jnp.broadcast_to(core == 0, (32, BLK))
    tail = pl.ds(HALF_COLS, 32)
    mine[tail, :] = jnp.where(first, ext[:, :BLK], ext[:, BLK:]).astype(BF16)
    other[tail, :] = jnp.where(first, ext[:, BLK:], ext[:, :BLK]).astype(BF16)


def head_rows(tail):
    tail = tail.astype(F32)
    return tail[0:8] + tail[8:16] + tail[16:24]


def logits_kernel(counts, own_low, own_high, a1, b1, a2, b2, a3, b3, iq0, iq1, iq2, iq3, *rest):
    logits_ref, stats_ref, latent_t, keys_out, keys_t_out, index_t, keys, total, own, sems = rest
    y, count = lax.axis_index("y"), slots_in_use(counts)
    half = SEL // 2
    loads = [
        pltpu.make_async_copy(own_low, own.at[pl.ds(0, half)], sems.at[2]),
        pltpu.make_async_copy(own_high, own.at[pl.ds(half, half)], sems.at[3]),
    ]
    for c in loads:
        c.start()
    for s, low, high in ((1, a1, b1), (2, a2, b2), (3, a3, b3), (0, own, own.at[pl.ds(half, half)])):
        if s == 0:
            for c in loads:
                c.wait()
        rows = pl.ds(pl.multiple_of(lax.rem(y + NY - s, NY) * PIECE, 16), PIECE)
        for j in range(half):
            keys[rows, j * BLK : (j + 1) * BLK] = low[j]
            keys[rows, (half + j) * BLK : (half + j + 1) * BLK] = high[j]
    copies = [pltpu.make_async_copy(keys.at[pl.ds(DK, ID), :], keys_out, sems.at[0])]
    copies[0].start()
    for j in range(SEL):
        span = slice(j * BLK, (j + 1) * BLK)
        latent_t[span, :] = keys[:DK, span].T
        index_t[span, :] = keys[DK:, span].T
    copies.append(pltpu.make_async_copy(index_t, keys_t_out, sems.at[1]))
    copies[1].start()
    iq_refs = (iq0, iq1, iq2, iq3)
    keys_t = index_t[pl.ds(pl.multiple_of(y * OWNK, OWNK), OWNK), :]
    total[...] = jnp.zeros_like(total)
    for ref in [r.at[n] for r in iq_refs for n in range(2)]:
        rows = head_rows(ref[HALF_COLS:, :])
        for p in range(4):
            a, b = 2 * p, 2 * p + 1
            pair = jnp.concatenate(
                [ref[a * ID : (a + 1) * ID, :], ref[b * ID : (b + 1) * ID, :]], axis=1
            )
            affinity = jnp.maximum(jnp.dot(keys_t, pair, preferred_element_type=F32), 0.0)
            total[...] += (
                affinity[:, :BLK] * rows[a : a + 1] + affinity[:, BLK:] * rows[b : b + 1]
            )
    key = lax.broadcasted_iota(I32, (OWNK, BLK), 0) + y * OWNK
    token = lax.broadcasted_iota(I32, (OWNK, BLK), 1)
    valid = (key < count * BLK) & ((key >= BLK) | (key <= token))
    masked = jnp.where(valid, total[...], masked_value)
    logits_ref[...] = masked
    peak = jnp.max(masked, axis=0, keepdims=True)
    mass = jnp.sum(jnp.exp(masked - peak), axis=0, keepdims=True)
    row = lax.broadcasted_iota(I32, (8, BLK), 0)
    stats_ref[...] = jnp.where(row == 0, peak, mass)
    for c in copies:
        c.wait()


def split_rows(row):
    hi = row.astype(BF16).astype(F32)
    mid = (row - hi).astype(BF16).astype(F32)
    return hi, mid, row - hi - mid


def tail_tile(rows):
    at = lax.broadcasted_iota(I32, (16, BLK), 0)
    tile = jnp.zeros((16, BLK), F32)
    for n, row in enumerate(rows):
        tile = jnp.where(at == n, row, tile)
    return tile.astype(BF16)


def target_kernel(
    counts, stats, keys_t, q_own, qb, o0, o1, o2, o3, qa, buf_a, buf_b, total, sem
):
    y, core, _ = place()
    count = slots_in_use(counts)
    lanes = pl.multiple_of(core * BLK, BLK)
    own = pltpu.make_async_copy(q_own.at[:, :, pl.ds(lanes, BLK)], qa, sem)
    own.start()
    total[...] = jnp.zeros_like(total)
    own.wait()

    chunk = 1024
    token = lax.broadcasted_iota(I32, (BLK, 2 * BLK), 1) % BLK
    causal = lax.broadcasted_iota(I32, (BLK, 2 * BLK), 0) <= token

    def rows_of(tile):
        return tile.reshape(tile.shape[0] // 8, 8, 2 * BLK)

    def score_part(pair, buf, k, peak):
        part = jnp.dot(keys_t[k * chunk : (k + 1) * chunk, :], pair, preferred_element_type=F32)
        for j in range(chunk // BLK):
            slot = k * (chunk // BLK) + j
            tile = part[j * BLK : (j + 1) * BLK]
            if slot == 0:
                tile = jnp.where(causal, tile, masked_value)
            buf[slot * BLK : (slot + 1) * BLK, :] = tile
            top = jnp.max(rows_of(tile), axis=0)
            peak = jnp.maximum(peak, jnp.where(slot < count, top, masked_value))
        return peak

    def exp_part(buf, k, shift, mass):
        span = slice(k * BLK, (k + 1) * BLK)
        tile = jnp.exp2(buf[span, :] * exp2_scale - shift)
        buf[span, :] = tile
        return mass + jnp.where(k < count, jnp.sum(rows_of(tile), axis=0), 0.0)

    def add_part(buf, k, share):
        span = slice(k * BLK, (k + 1) * BLK)
        tile = buf[span, :] * share
        total[span, :] += tile[:, :BLK] + tile[:, BLK:]

    low = jnp.full((8, 2 * BLK), masked_value, F32)
    parts = KEYS // chunk
    step_slots = SEL // (parts // 2)

    def both(p, buf, done, shift):
        peak = low
        if p is not None:
            pair = jnp.concatenate([qa[p], qb[p]], axis=1)
        mass = jnp.zeros((8, 2 * BLK), F32)
        for k in range(parts // 2):
            if p is not None:
                peak = score_part(pair, buf, k, peak)
            if done is not None:
                for n in range(step_slots * k, step_slots * (k + 1)):
                    mass = exp_part(done, n, shift, mass)
        if done is not None:
            share = 1.0 / (jnp.sum(mass, axis=0, keepdims=True) * H)
        for k in range(parts // 2):
            if p is not None:
                peak = score_part(pair, buf, parts // 2 + k, peak)
            if done is not None:
                for n in range(step_slots * k, step_slots * (k + 1)):
                    add_part(done, n, share)
        return jnp.max(peak, axis=0, keepdims=True) * exp2_scale

    def step(k, shift):
        shift = both(2 * k + 1, buf_b, buf_a, shift)
        return both(2 * k + 2, buf_a, buf_b, shift)

    pairs = qa.shape[0]
    shift = both(0, buf_a, None, None)
    shift = lax.fori_loop(0, pairs // 2 - 1, step, shift)
    shift = both(pairs - 1, buf_b, buf_a, shift)
    both(None, None, buf_b, shift)
    tail = tail_tile(split_rows(stats[0:1, :]) + split_rows(stats[1:2, :]))
    for s, out in enumerate((o0, o1, o2, o3)):
        start = pl.multiple_of(lax.rem(y + s, NY) * OWNK, OWNK)
        used = lax.broadcasted_iota(I32, (OWNK, BLK), 0) + start < count * BLK
        out[:OWNK, :] = jnp.where(used, total[pl.ds(start, OWNK), :], 0.0).astype(BF16)
        out[OWNK:, :] = tail


def loss_kernel(t0, t1, t2, t3, logits, out):
    pieces = (t0, t1, t2, t3)
    tails = [t[OWNK:, :].astype(F32) for t in pieces]
    peaks = [t[0:1] + t[1:2] + t[2:3] for t in tails]
    masses = [t[3:4] + t[4:5] + t[5:6] for t in tails]
    peak = functools.reduce(jnp.maximum, peaks)
    mass = functools.reduce(jnp.add, [m * jnp.exp(p - peak) for m, p in zip(masses, peaks)])
    log_total = peak + jnp.log(mass)
    target = functools.reduce(jnp.add, [t[:OWNK, :].astype(F32) for t in pieces])
    masked = logits[...]
    valid = masked > 0.5 * masked_value
    log_probs = masked - log_total
    entropy = -jnp.sum(jnp.where(valid, target * log_probs, 0.0), axis=0, keepdims=True)
    grad = jnp.where(valid, jnp.exp(log_probs) - target, 0.0) / QUERIES
    out[:OWNK, :] = grad.astype(BF16)
    out[OWNK:, :] = tail_tile(split_rows(entropy))


def backward_kernel(g0, g1, g2, g3, keys, keys_t, iq, out, entropy_ref, grads):
    y = lax.axis_index("y")
    entropy = jnp.zeros((1, BLK), F32)
    for s, piece in enumerate((g0, g1, g2, g3)):
        start = pl.multiple_of(lax.rem(y + NY - s, NY) * OWNK, OWNK)
        grads[pl.ds(start, OWNK), :] = piece[:OWNK, :].astype(F32)
        tail = piece[OWNK:, :].astype(F32)
        entropy = entropy + tail[0:1] + tail[1:2] + tail[2:3]
    entropy_ref[...] = jnp.broadcast_to(entropy, (8, BLK))
    chunk = 512
    for core in range(2):
        ref = iq.at[core]
        rows = head_rows(ref[HALF_COLS:, :])
        for p in range(4):
            a, b = 2 * p, 2 * p + 1
            pair = jnp.concatenate(
                [ref[a * ID : (a + 1) * ID, :], ref[b * ID : (b + 1) * ID, :]], axis=1
            )
            acc = jnp.zeros((ID, 2 * BLK), F32)
            for k in range(KEYS // chunk):
                span = slice(k * chunk, (k + 1) * chunk)
                affinity = jnp.dot(keys_t[span, :], pair, preferred_element_type=F32)
                grad = grads[span, :]
                scaled = jnp.concatenate([grad * rows[a : a + 1], grad * rows[b : b + 1]], axis=1)
                masked = jnp.where(affinity > 0, scaled, 0.0).astype(BF16)
                acc = acc + jnp.dot(keys[:, span], masked, preferred_element_type=F32)
            acc = acc.astype(BF16)
            for n, head in enumerate((a, b)):
                lanes = slice(n * BLK, (n + 1) * BLK)
                out[2 * owner_of_piece(2 * head) + core] = acc[:COLS, lanes]
                out[2 * owner_of_piece(2 * head + 1) + core] = acc[COLS:, lanes]


def owner_of_piece(piece):
    k, x = piece // 4, piece % 4
    return (k - 2 * x) % 4 * 4 + x


def weight_kernel(qg, xa, xb, out, lhs, own_x, sems):
    parts = sems.shape[0]
    span = QUERIES // parts
    copies = []
    for k in range(parts):
        rows = pl.ds(k * span, span)
        copies.append(pltpu.make_async_copy(xa.at[rows, :], own_x.at[rows, :], sems.at[k]))
        copies[-1].start()
    for s in range(2 * NQ):
        lhs[:, s * BLK : (s + 1) * BLK] = qg[s]
    other = jnp.dot(lhs[...], xb[...], preferred_element_type=F32).astype(BF16)
    own = jnp.zeros(other.shape, F32)
    for k in range(parts):
        rows = slice(k * span, (k + 1) * span)
        copies[k].wait()
        own = own + jnp.dot(lhs[:, rows], own_x[rows, :], preferred_element_type=F32)
    own = own.astype(BF16)
    own_first = jnp.broadcast_to(lax.axis_index("c") == 0, own.shape)
    half = own.shape[1]
    out[:, :half] = jnp.where(own_first, own, other)
    out[:, half:] = jnp.where(own_first, other, own)


def quarter_kernel(p0, p1, p2, p3, full, top, bottom, rows):
    x = lax.axis_index("x")
    for s, piece in enumerate((p0, p1, p2, p3)):
        start = pl.multiple_of(lax.rem(x + 4 - s, 4) * COLS, COLS)
        rows[pl.ds(start, COLS), :] = piece[...]
    for k in range(6):
        tile = rows[:, k * 256 : (k + 1) * 256].T
        full[k * 256 : (k + 1) * 256, :] = tile
        half = top if k < 3 else bottom
        half[k % 3 * 256 : (k % 3 + 1) * 256, :] = tile


def finish_kernel(own, below, above, top, bottom, out, wide, sems):
    colour = lax.rem(lax.axis_index("z") + 2 * lax.axis_index("x"), 4)
    half = DQ // 2
    copies = []
    for n, (shift, pieces) in enumerate(
        ((0, (own,)), (2, (top, bottom)), (3, (below,)), (1, (above,)))
    ):
        for m, piece in enumerate(pieces):
            wide[n, m * half : m * half + piece.shape[0], :] = piece[...].astype(F32)
        lanes = pl.multiple_of(lax.rem(colour + shift, 4) * 256, 256)
        copies.append(pltpu.make_async_copy(wide.at[n], out.at[:, pl.ds(lanes, 256)], sems.at[n]))
        copies[-1].start()
    for c in copies:
        c.wait()


def plane(dz, dx):
    return [
        (z * 4 + x, (z + dz) % 4 * 4 + (x + dx) % 4) for z in range(4) for x in range(4)
    ]


def ring(shift):
    return [(i, (i + shift) % NY) for i in range(NY)]


SWAP = [(0, 1), (1, 0)]
SHIFTS = (1, 3, 2)


def around_y(array):
    moved = {s: lax.ppermute(array, "y", ring(s)) for s in SHIFTS}
    return (array, moved[1], moved[2], moved[3])


def on_device(
    q_absorbed, key_cache, index_input, index_weight, head_weights, block_ids, block_counts
):
    y, core, _ = place()
    ids = block_ids.T

    outgoing = call(
        pick_outgoing_kernel,
        shape((NQ * CAP, PIECE, BLK), BF16),
        [SMEM, ANY],
        VMEM,
        [pltpu.SMEM((NQ * SEL + 1,), I32), pltpu.SemaphoreType.DMA],
        "pick_outgoing",
    )(ids, in_hbm(key_cache))
    arrived = lax.all_to_all(outgoing, ("z", "x"), split_axis=0, concat_axis=0, tiled=True)

    iq_own, iq_send = call(
        index_query_kernel,
        (shape((IQ_ROWS, BLK), BF16),) * 2,
        [VMEM, VMEM, VMEM],
        (VMEM, VMEM),
        name="index_query",
    )(index_input, index_weight, head_weights.T)
    iq_other = lax.ppermute(iq_send, "c", SWAP)
    first = core == 0
    iq_pair = jnp.stack(
        [jnp.where(first, iq_own, iq_other), jnp.where(first, iq_other, iq_own)]
    )
    iq_all = around_y(iq_pair)

    q_t = jnp.transpose(q_absorbed, (1, 2, 0))
    q_send = lax.dynamic_slice_in_dim(q_t, (1 - core) * BLK, BLK, 2)
    q_other = lax.ppermute(q_send, "c", SWAP)

    low, high = call(
        pick_listed_kernel,
        (pltpu.HBM((SEL // 2, PIECE, BLK), BF16),) * 2,
        [SMEM] + [ANY] * 5,
        (HBM, HBM),
        [
            pltpu.VMEM((SEL, PIECE, BLK), BF16),
            pltpu.SMEM((NQ,), I32),
            pltpu.SemaphoreType.DMA((2,)),
        ],
        "pick_listed",
    )(ids, arrived, q_send, *iq_all[1:])
    low_up, high_down = lax.ppermute(low, "y", ring(1)), lax.ppermute(high, "y", ring(3))
    high_up, low_down = lax.ppermute(high, "y", ring(1)), lax.ppermute(low, "y", ring(3))
    low_far, high_far = lax.ppermute(low_up, "y", ring(1)), lax.ppermute(high_down, "y", ring(3))
    moved = (low_up, high_up, low_far, high_far, low_down, high_down)

    half = DQ // 2
    x_half = lax.dynamic_slice_in_dim(index_input, core * half, half, 1)
    x_half, _ = lax.optimization_barrier((x_half, low))
    x_own = lax.all_gather(x_half, ("z", "x"), axis=0, tiled=True)

    logits, stats, latent_t, index_keys, index_t = call(
        logits_kernel,
        (
            shape((OWNK, BLK), F32),
            shape((8, BLK), F32),
            shape((KEYS, DK), BF16),
            pltpu.HBM((ID, KEYS), BF16),
            pltpu.HBM((KEYS, ID), BF16),
        ),
        [SMEM, ANY, ANY] + [VMEM] * 10,
        (VMEM, VMEM, VMEM, HBM, HBM),
        [
            pltpu.VMEM((KEYS, ID), BF16),
            pltpu.VMEM((DK + ID, KEYS), BF16),
            pltpu.VMEM((OWNK, BLK), F32),
            pltpu.VMEM((SEL, PIECE, BLK), BF16),
            pltpu.SemaphoreType.DMA((4,)),
        ],
        "index_logits",
    )(block_counts, in_hbm(low), in_hbm(high), *map(in_vmem, (*moved, *iq_all)))

    targets = call(
        target_kernel,
        (shape((LG_ROWS, BLK), BF16),) * 4,
        [SMEM, VMEM, VMEM, ANY, VMEM],
        (VMEM,) * 4,
        [
            pltpu.VMEM((16, DK, BLK), BF16),
            pltpu.VMEM((KEYS, 2 * BLK), F32),
            pltpu.VMEM((KEYS, 2 * BLK), F32),
            pltpu.VMEM((KEYS, BLK), F32),
            pltpu.SemaphoreType.DMA,
        ],
        "attention_target",
    )(block_counts, stats, in_vmem(latent_t), in_hbm(q_t), in_vmem(q_other))
    arrived_targets = {s: lax.ppermute(targets[s], "y", ring(s)) for s in SHIFTS}

    grads = call(
        loss_kernel,
        shape((LG_ROWS, BLK), BF16),
        [VMEM] * 5,
        VMEM,
        name="loss",
    )(*map(in_vmem, (targets[0], *(arrived_targets[s] for s in (1, 2, 3)), logits)))
    x_own, _ = lax.optimization_barrier((x_own, grads))
    x_other = lax.ppermute(x_own, "c", SWAP)
    grads_all = around_y(grads)

    query_grad, entropy = call(
        backward_kernel,
        (shape((2 * NQ, COLS, BLK), BF16), shape((8, BLK), F32)),
        [VMEM] * 7,
        (VMEM, VMEM),
        [pltpu.VMEM((KEYS, BLK), F32)],
        "index_backward",
    )(*map(in_vmem, (*grads_all, index_keys, index_t, iq_pair)))
    entropy_other = lax.ppermute(entropy, "c", SWAP)
    entropy_both = jnp.where(
        first,
        jnp.concatenate([entropy[0], entropy_other[0]]),
        jnp.concatenate([entropy_other[0], entropy[0]]),
    )
    share = 2 * BLK // (2 * NY)
    entropy_mine = lax.dynamic_slice_in_dim(entropy_both, (2 * y + core) * share, share, 0)

    swapped = lax.all_to_all(query_grad, ("z", "x", "c"), split_axis=0, concat_axis=0, tiled=True)
    qblk = ("z", "x")
    piece = call(
        weight_kernel,
        shape((COLS, DQ), BF16),
        [VMEM, ANY, VMEM],
        VMEM,
        [
            pltpu.VMEM((COLS, QUERIES), BF16),
            pltpu.VMEM((QUERIES, half), BF16),
            pltpu.SemaphoreType.DMA((4,)),
        ],
        "weight_piece",
    )(in_vmem(swapped), in_hbm(x_own), in_vmem(x_other))
    same = [piece] + [lax.ppermute(piece, qblk, plane(-2 * d, d)) for d in (1, 2, 3)]
    full, top, bottom = call(
        quarter_kernel,
        (shape((DQ, 256), BF16), shape((half, 256), BF16), shape((half, 256), BF16)),
        [VMEM] * 4,
        (VMEM,) * 3,
        [pltpu.VMEM((256, DQ), BF16)],
        "quarter",
    )(*map(in_vmem, same))
    below = lax.ppermute(full, qblk, plane(1, 0))
    above = lax.ppermute(full, qblk, plane(-1, 0))
    top = lax.ppermute(top, qblk, plane(0, -1))
    bottom = lax.ppermute(bottom, qblk, plane(0, 1))
    weight_grad = call(
        finish_kernel,
        shape((DQ, HALF_COLS), F32),
        [VMEM] * 5,
        ANY,
        [pltpu.VMEM((4, DQ, 256), F32), pltpu.SemaphoreType.DMA((4,))],
        "finish",
    )(*map(in_vmem, (full, below, above, top, bottom)))
    return weight_grad, entropy_mine


def solution(mesh):
    fine = Mesh(mesh.devices.reshape(NY, 2, 4, 4), ("y", "c", "z", "x"))
    head, qblk = ("y", "c"), ("z", "x")
    placed = (
        P(qblk, head, None),
        P(qblk, None, None),
        P(qblk, None),
        P(None, head),
        P(qblk, head),
        P(),
        P(),
    )
    return jax.shard_map(
        on_device,
        mesh=fine,
        in_specs=placed,
        out_specs=(P(None, head), P(qblk + head)),
        check_vma=False,
    )
```

```python
import functools

import jax
import jax.numpy as jnp
from jax import lax
from jax.experimental import pallas as pl
from jax.experimental.pallas import tpu as pltpu
from jax.sharding import Mesh, PartitionSpec as P

BF16 = jnp.bfloat16
F32 = jnp.float32
I32 = jnp.int32

H = 128
DK = 576
ID = 128
CAP = 3
BLK = 128
SEL = 16
KEYS = SEL * BLK
NY = 4
NQ = 16
SHARD = 32
LATC = DK // NY
IDXC = ID // NY
PIECE = LATC + IDXC
OWNK = KEYS // NY
HALF_COLS = 1024
IQ_ROWS = HALF_COLS + 32
LG_ROWS = OWNK + 16
DQ = 1536
COLS = HALF_COLS // NQ
QUERIES = 4096

score_scale = 192.0 ** (-0.5)
exp2_scale = score_scale * 1.4426950408889634
masked_value = -1e30
VMEM_LIMIT = 24 * 1024 * 1024

ANY = pl.BlockSpec(memory_space=pl.ANY)
VMEM = pl.BlockSpec(memory_space=pltpu.VMEM)
SMEM = pl.BlockSpec(memory_space=pltpu.SMEM)
HBM = pl.BlockSpec(memory_space=pltpu.HBM)


def call(kernel, out_shape, in_specs, out_specs, scratch=(), name=None, aliases=None):
    return pl.pallas_call(
        kernel,
        out_shape=out_shape,
        in_specs=in_specs,
        out_specs=out_specs,
        scratch_shapes=list(scratch),
        compiler_params=pltpu.CompilerParams(vmem_limit_bytes=VMEM_LIMIT),
        name=name,
        input_output_aliases=aliases or {},
    )


def shape(dims, dtype):
    return jax.ShapeDtypeStruct(dims, dtype)


def in_hbm(array):
    return pltpu.with_memory_space_constraint(array, pltpu.HBM)


def in_vmem(array):
    return pltpu.with_memory_space_constraint(array, pltpu.VMEM)


def place():
    return lax.axis_index("y"), lax.axis_index("c"), lax.axis_index(("z", "x"))


def slots_in_use(counts):
    _, core, me = place()
    return counts[2 * me + core]


def pick_outgoing_kernel(ids, cache, out, found, sem):
    y, core, me = place()
    rows = pl.ds(pl.multiple_of(y * PIECE, 16), PIECE)
    first = me * SHARD

    def copy(block, place_out):
        return pltpu.make_async_copy(cache.at[block, rows, :], out.at[place_out], sem)

    def per_dst(dst, total):
        count = jnp.int32(0)
        for s in range(SEL):
            local = ids[s, 2 * dst + core] - first
            found[total + count] = local * (NQ * CAP) + dst * CAP + jnp.minimum(count, CAP - 1)
            count = count + ((local >= 0) & (local < SHARD)).astype(I32)
        return total + count

    total = lax.fori_loop(0, NQ, per_dst, jnp.int32(0))

    def start(n, carry):
        code = found[n]
        block = code // (NQ * CAP)
        copy(block, code - block * (NQ * CAP)).start()
        return carry

    def wait(n, carry):
        copy(0, 0).wait()
        return carry

    lax.fori_loop(0, total, start, 0)
    lax.fori_loop(0, total, wait, 0)


def pick_listed_kernel(ids, arrived, *refs):
    low, high, listed, seen, sem = refs[-5:]
    _, core, me = place()
    row = 2 * me + core
    for i in range(NQ):
        seen[i] = 0
    pending = []
    for s in range(SEL):
        owner = lax.shift_right_logical(ids[s, row], 5)
        rank = jnp.minimum(seen[owner], CAP - 1)
        seen[owner] = seen[owner] + 1
        pending.append(pltpu.make_async_copy(arrived.at[owner * CAP + rank], listed.at[s], sem.at[0]))
        pending[-1].start()
    for c in pending:
        c.wait()
    half = SEL // 2
    outs = [
        pltpu.make_async_copy(listed.at[pl.ds(n * half, half)], out, sem.at[1])
        for n, out in enumerate((low, high))
    ]
    for c in outs:
        c.start()
    for c in outs:
        c.wait()


def index_query_kernel(x, w, hw, mine, other):
    core = lax.axis_index("c")
    for k in range(4):
        cols = HALF_COLS // 4
        part = jnp.dot(x[...], w[:, k * cols : (k + 1) * cols], preferred_element_type=F32)
        part = part.astype(BF16)
        low = part[:BLK].T
        high = part[BLK:].T
        rows = pl.ds(k * cols, cols)
        first = jnp.broadcast_to(core == 0, low.shape)
        mine[rows, :] = jnp.where(first, low, high)
        other[rows, :] = jnp.where(first, high, low)
    weights = hw[...]
    hi = weights.astype(BF16)
    rest = weights - hi.astype(F32)
    mid = rest.astype(BF16)
    lo = (rest - mid.astype(F32)).astype(BF16)
    ext = jnp.concatenate(
        [hi.astype(F32), mid.astype(F32), lo.astype(F32), jnp.zeros_like(weights)], axis=0
    )
    first = jnp.broadcast_to(core == 0, (32, BLK))
    tail = pl.ds(HALF_COLS, 32)
    mine[tail, :] = jnp.where(first, ext[:, :BLK], ext[:, BLK:]).astype(BF16)
    other[tail, :] = jnp.where(first, ext[:, BLK:], ext[:, :BLK]).astype(BF16)


def head_rows(tail):
    tail = tail.astype(F32)
    return tail[0:8] + tail[8:16] + tail[16:24]


def logits_kernel(counts, own_low, own_high, a1, b1, a2, b2, a3, b3, *refs):
    iq_refs, rest = refs[:8], refs[8:]
    logits_ref, stats_ref, latent_t, keys_out, keys_t_out, index_t, keys, total, own, sems = rest
    y, count = lax.axis_index("y"), slots_in_use(counts)
    half = SEL // 2
    loads = [
        pltpu.make_async_copy(own_low, own.at[pl.ds(0, half)], sems.at[2]),
        pltpu.make_async_copy(own_high, own.at[pl.ds(half, half)], sems.at[3]),
    ]
    for c in loads:
        c.start()
    for s, low, high in ((1, a1, b1), (2, a2, b2), (3, a3, b3), (0, own, own.at[pl.ds(half, half)])):
        if s == 0:
            for c in loads:
                c.wait()
        rows = pl.ds(pl.multiple_of(lax.rem(y + NY - s, NY) * PIECE, 16), PIECE)
        for j in range(half):
            keys[rows, j * BLK : (j + 1) * BLK] = low[j]
            keys[rows, (half + j) * BLK : (half + j + 1) * BLK] = high[j]
    copies = [pltpu.make_async_copy(keys.at[pl.ds(DK, ID), :], keys_out, sems.at[0])]
    copies[0].start()
    for j in range(SEL):
        span = slice(j * BLK, (j + 1) * BLK)
        latent_t[span, :] = keys[:DK, span].T
        index_t[span, :] = keys[DK:, span].T
    copies.append(pltpu.make_async_copy(index_t, keys_t_out, sems.at[1]))
    copies[1].start()
    keys_t = index_t[pl.ds(pl.multiple_of(y * OWNK, OWNK), OWNK), :]
    total[...] = jnp.zeros_like(total)
    for ref in iq_refs:
        rows = head_rows(ref[HALF_COLS:, :])
        for p in range(4):
            a, b = 2 * p, 2 * p + 1
            pair = jnp.concatenate(
                [ref[a * ID : (a + 1) * ID, :], ref[b * ID : (b + 1) * ID, :]], axis=1
            )
            affinity = jnp.maximum(jnp.dot(keys_t, pair, preferred_element_type=F32), 0.0)
            total[...] += (
                affinity[:, :BLK] * rows[a : a + 1] + affinity[:, BLK:] * rows[b : b + 1]
            )
    key = lax.broadcasted_iota(I32, (OWNK, BLK), 0) + y * OWNK
    token = lax.broadcasted_iota(I32, (OWNK, BLK), 1)
    valid = (key < count * BLK) & ((key >= BLK) | (key <= token))
    masked = jnp.where(valid, total[...], masked_value)
    logits_ref[...] = masked
    peak = jnp.max(masked, axis=0, keepdims=True)
    mass = jnp.sum(jnp.exp(masked - peak), axis=0, keepdims=True)
    row = lax.broadcasted_iota(I32, (8, BLK), 0)
    stats_ref[...] = jnp.where(row == 0, peak, mass)
    for c in copies:
        c.wait()


def split_rows(row):
    hi = row.astype(BF16).astype(F32)
    mid = (row - hi).astype(BF16).astype(F32)
    return hi, mid, row - hi - mid


def tail_tile(rows):
    at = lax.broadcasted_iota(I32, (16, BLK), 0)
    tile = jnp.zeros((16, BLK), F32)
    for n, row in enumerate(rows):
        tile = jnp.where(at == n, row, tile)
    return tile.astype(BF16)


def target_kernel(
    counts, stats, keys_t, q_own, qb, o0, o1, o2, o3, qa, buf_a, buf_b, total, sem
):
    y, core, _ = place()
    count = slots_in_use(counts)
    lanes = pl.multiple_of(core * BLK, BLK)
    own = pltpu.make_async_copy(q_own.at[:, :, pl.ds(lanes, BLK)], qa, sem)
    own.start()
    total[...] = jnp.zeros_like(total)
    own.wait()

    chunk = 1024
    token = lax.broadcasted_iota(I32, (BLK, 2 * BLK), 1) % BLK
    causal = lax.broadcasted_iota(I32, (BLK, 2 * BLK), 0) <= token

    def rows_of(tile):
        return tile.reshape(tile.shape[0] // 8, 8, 2 * BLK)

    def score_part(pair, buf, k, peak):
        part = jnp.dot(keys_t[k * chunk : (k + 1) * chunk, :], pair, preferred_element_type=F32)
        for j in range(chunk // BLK):
            slot = k * (chunk // BLK) + j
            tile = part[j * BLK : (j + 1) * BLK]
            if slot == 0:
                tile = jnp.where(causal, tile, masked_value)
            buf[slot * BLK : (slot + 1) * BLK, :] = tile
            top = jnp.max(rows_of(tile), axis=0)
            peak = jnp.maximum(peak, jnp.where(slot < count, top, masked_value))
        return peak

    def exp_part(buf, k, shift, mass):
        span = slice(k * BLK, (k + 1) * BLK)
        tile = jnp.exp2(buf[span, :] * exp2_scale - shift)
        buf[span, :] = tile
        return mass + jnp.where(k < count, jnp.sum(rows_of(tile), axis=0), 0.0)

    def add_part(buf, k, share):
        span = slice(k * BLK, (k + 1) * BLK)
        tile = buf[span, :] * share
        total[span, :] += tile[:, :BLK] + tile[:, BLK:]

    low = jnp.full((8, 2 * BLK), masked_value, F32)
    parts = KEYS // chunk
    step_slots = SEL // (parts // 2)

    def both(p, buf, done, shift):
        peak = low
        if p is not None:
            pair = jnp.concatenate([qa[p], qb[p]], axis=1)
        mass = jnp.zeros((8, 2 * BLK), F32)
        for k in range(parts // 2):
            if p is not None:
                peak = score_part(pair, buf, k, peak)
            if done is not None:
                for n in range(step_slots * k, step_slots * (k + 1)):
                    mass = exp_part(done, n, shift, mass)
        if done is not None:
            share = 1.0 / (jnp.sum(mass, axis=0, keepdims=True) * H)
        for k in range(parts // 2):
            if p is not None:
                peak = score_part(pair, buf, parts // 2 + k, peak)
            if done is not None:
                for n in range(step_slots * k, step_slots * (k + 1)):
                    add_part(done, n, share)
        return jnp.max(peak, axis=0, keepdims=True) * exp2_scale

    def step(k, shift):
        shift = both(2 * k + 1, buf_b, buf_a, shift)
        return both(2 * k + 2, buf_a, buf_b, shift)

    pairs = qa.shape[0]
    shift = both(0, buf_a, None, None)
    shift = lax.fori_loop(0, pairs // 2 - 1, step, shift)
    shift = both(pairs - 1, buf_b, buf_a, shift)
    both(None, None, buf_b, shift)
    tail = tail_tile(split_rows(stats[0:1, :]) + split_rows(stats[1:2, :]))
    for s, out in enumerate((o0, o1, o2, o3)):
        start = pl.multiple_of(lax.rem(y + s, NY) * OWNK, OWNK)
        used = lax.broadcasted_iota(I32, (OWNK, BLK), 0) + start < count * BLK
        out[:OWNK, :] = jnp.where(used, total[pl.ds(start, OWNK), :], 0.0).astype(BF16)
        out[OWNK:, :] = tail


def loss_kernel(t0, t1, t2, t3, logits, out):
    pieces = (t0, t1, t2, t3)
    tails = [t[OWNK:, :].astype(F32) for t in pieces]
    peaks = [t[0:1] + t[1:2] + t[2:3] for t in tails]
    masses = [t[3:4] + t[4:5] + t[5:6] for t in tails]
    peak = functools.reduce(jnp.maximum, peaks)
    mass = functools.reduce(jnp.add, [m * jnp.exp(p - peak) for m, p in zip(masses, peaks)])
    log_total = peak + jnp.log(mass)
    target = functools.reduce(jnp.add, [t[:OWNK, :].astype(F32) for t in pieces])
    masked = logits[...]
    valid = masked > 0.5 * masked_value
    log_probs = masked - log_total
    entropy = -jnp.sum(jnp.where(valid, target * log_probs, 0.0), axis=0, keepdims=True)
    grad = jnp.where(valid, jnp.exp(log_probs) - target, 0.0) / QUERIES
    out[:OWNK, :] = grad.astype(BF16)
    out[OWNK:, :] = tail_tile(split_rows(entropy))


def backward_kernel(g0, g1, g2, g3, keys, keys_t, iq_first, iq_second, out, entropy_ref, grads):
    y = lax.axis_index("y")
    entropy = jnp.zeros((1, BLK), F32)
    for s, piece in enumerate((g0, g1, g2, g3)):
        start = pl.multiple_of(lax.rem(y + NY - s, NY) * OWNK, OWNK)
        grads[pl.ds(start, OWNK), :] = piece[:OWNK, :].astype(F32)
        tail = piece[OWNK:, :].astype(F32)
        entropy = entropy + tail[0:1] + tail[1:2] + tail[2:3]
    entropy_ref[...] = jnp.broadcast_to(entropy, (8, BLK))
    chunk = 512
    for core, ref in enumerate((iq_first, iq_second)):
        rows = head_rows(ref[HALF_COLS:, :])
        for p in range(4):
            a, b = 2 * p, 2 * p + 1
            pair = jnp.concatenate(
                [ref[a * ID : (a + 1) * ID, :], ref[b * ID : (b + 1) * ID, :]], axis=1
            )
            acc = jnp.zeros((ID, 2 * BLK), F32)
            for k in range(KEYS // chunk):
                span = slice(k * chunk, (k + 1) * chunk)
                affinity = jnp.dot(keys_t[span, :], pair, preferred_element_type=F32)
                grad = grads[span, :]
                scaled = jnp.concatenate([grad * rows[a : a + 1], grad * rows[b : b + 1]], axis=1)
                masked = jnp.where(affinity > 0, scaled, 0.0).astype(BF16)
                acc = acc + jnp.dot(keys[:, span], masked, preferred_element_type=F32)
            acc = acc.astype(BF16)
            for n, head in enumerate((a, b)):
                lanes = slice(n * BLK, (n + 1) * BLK)
                out[2 * owner_of_piece(2 * head) + core] = acc[:COLS, lanes]
                out[2 * owner_of_piece(2 * head + 1) + core] = acc[COLS:, lanes]


def owner_of_piece(piece):
    k, x = piece // 4, piece % 4
    return (k - 2 * x) % 4 * 4 + x


def weight_kernel(qg, xa, xb, out, lhs, own_x, sems):
    parts = sems.shape[0]
    span = QUERIES // parts
    copies = []
    for k in range(parts):
        rows = pl.ds(k * span, span)
        copies.append(pltpu.make_async_copy(xa.at[rows, :], own_x.at[rows, :], sems.at[k]))
        copies[-1].start()
    for s in range(2 * NQ):
        lhs[:, s * BLK : (s + 1) * BLK] = qg[s]
    other = jnp.dot(lhs[...], xb[...], preferred_element_type=F32).astype(BF16)
    own = jnp.zeros(other.shape, F32)
    for k in range(parts):
        rows = slice(k * span, (k + 1) * span)
        copies[k].wait()
        own = own + jnp.dot(lhs[:, rows], own_x[rows, :], preferred_element_type=F32)
    own = own.astype(BF16)
    own_first = jnp.broadcast_to(lax.axis_index("c") == 0, own.shape)
    half = own.shape[1]
    out[:, :half] = jnp.where(own_first, own, other)
    out[:, half:] = jnp.where(own_first, other, own)


def quarter_kernel(p0, p1, p2, p3, full, top, bottom, rows):
    x = lax.axis_index("x")
    for s, piece in enumerate((p0, p1, p2, p3)):
        start = pl.multiple_of(lax.rem(x + 4 - s, 4) * COLS, COLS)
        rows[pl.ds(start, COLS), :] = piece[...]
    for k in range(6):
        tile = rows[:, k * 256 : (k + 1) * 256].T
        full[k * 256 : (k + 1) * 256, :] = tile
        half = top if k < 3 else bottom
        half[k % 3 * 256 : (k % 3 + 1) * 256, :] = tile


def finish_kernel(shifts, *refs):
    pieces, (out, wide, sems) = refs[:-3], refs[-3:]
    colour = lax.rem(lax.axis_index("z") + 2 * lax.axis_index("x"), 4)
    copies, at = [], 0
    for n, shift in enumerate(shifts):
        row = 0
        while row < DQ:
            piece = pieces[at]
            wide[n, row : row + piece.shape[0], :] = piece[...].astype(F32)
            row, at = row + piece.shape[0], at + 1
        lanes = pl.multiple_of(lax.rem(colour + shift, 4) * 256, 256)
        copies.append(pltpu.make_async_copy(wide.at[n], out.at[:, pl.ds(lanes, 256)], sems.at[n]))
        copies[-1].start()
    for c in copies:
        c.wait()


def finish_rest_kernel(started, *refs):
    del started
    finish_kernel((3, 1), *refs)


def plane(dz, dx):
    return [
        (z * 4 + x, (z + dz) % 4 * 4 + (x + dx) % 4) for z in range(4) for x in range(4)
    ]


def ring(shift):
    return [(i, (i + shift) % NY) for i in range(NY)]


SWAP = [(0, 1), (1, 0)]
SHIFTS = (1, 3, 2)


def relayed(low, high):
    low_up, high_down = lax.ppermute(low, "y", ring(1)), lax.ppermute(high, "y", ring(3))
    high_up, low_down = lax.ppermute(high, "y", ring(1)), lax.ppermute(low, "y", ring(3))
    low_far, high_far = lax.ppermute(low_up, "y", ring(1)), lax.ppermute(high_down, "y", ring(3))
    return low_up, high_up, low_far, high_far, low_down, high_down


def around_y(array):
    moved = {s: lax.ppermute(array, "y", ring(s)) for s in SHIFTS}
    return (array, moved[1], moved[2], moved[3])


def on_device(
    q_absorbed, key_cache, index_input, index_weight, head_weights, block_ids, block_counts
):
    y, core, _ = place()
    ids = block_ids.T

    outgoing = call(
        pick_outgoing_kernel,
        shape((NQ * CAP, PIECE, BLK), BF16),
        [SMEM, ANY],
        VMEM,
        [pltpu.SMEM((NQ * SEL + 1,), I32), pltpu.SemaphoreType.DMA],
        "pick_outgoing",
    )(ids, in_hbm(key_cache))
    arrived = lax.all_to_all(outgoing, ("z", "x"), split_axis=0, concat_axis=0, tiled=True)

    iq_own, iq_send = call(
        index_query_kernel,
        (shape((IQ_ROWS, BLK), BF16),) * 2,
        [VMEM, VMEM, VMEM],
        (VMEM, VMEM),
        name="index_query",
    )(index_input, index_weight, head_weights.T)
    iq_other = lax.ppermute(iq_send, "c", SWAP)
    first = core == 0
    iq_pair = (jnp.where(first, iq_own, iq_other), jnp.where(first, iq_other, iq_own))
    iq_moved = relayed(*iq_pair)

    q_t = jnp.transpose(q_absorbed, (1, 2, 0))
    q_send = lax.dynamic_slice_in_dim(q_t, (1 - core) * BLK, BLK, 2)
    q_other = lax.ppermute(q_send, "c", SWAP)

    low, high = call(
        pick_listed_kernel,
        (pltpu.HBM((SEL // 2, PIECE, BLK), BF16),) * 2,
        [SMEM] + [ANY] * 8,
        (HBM, HBM),
        [
            pltpu.VMEM((SEL, PIECE, BLK), BF16),
            pltpu.SMEM((NQ,), I32),
            pltpu.SemaphoreType.DMA((2,)),
        ],
        "pick_listed",
    )(ids, arrived, q_send, *iq_moved)
    moved = relayed(low, high)

    half = DQ // 2
    x_half = lax.dynamic_slice_in_dim(index_input, core * half, half, 1)
    x_half, _ = lax.optimization_barrier((x_half, low))
    x_own = lax.all_gather(x_half, ("z", "x"), axis=0, tiled=True)

    logits, stats, latent_t, index_keys, index_t = call(
        logits_kernel,
        (
            shape((OWNK, BLK), F32),
            shape((8, BLK), F32),
            shape((KEYS, DK), BF16),
            pltpu.HBM((ID, KEYS), BF16),
            pltpu.HBM((KEYS, ID), BF16),
        ),
        [SMEM, ANY, ANY] + [VMEM] * 14,
        (VMEM, VMEM, VMEM, HBM, HBM),
        [
            pltpu.VMEM((KEYS, ID), BF16),
            pltpu.VMEM((DK + ID, KEYS), BF16),
            pltpu.VMEM((OWNK, BLK), F32),
            pltpu.VMEM((SEL, PIECE, BLK), BF16),
            pltpu.SemaphoreType.DMA((4,)),
        ],
        "index_logits",
    )(block_counts, in_hbm(low), in_hbm(high), *map(in_vmem, (*moved, *iq_pair, *iq_moved)))

    targets = call(
        target_kernel,
        (shape((LG_ROWS, BLK), BF16),) * 4,
        [SMEM, VMEM, VMEM, ANY, VMEM],
        (VMEM,) * 4,
        [
            pltpu.VMEM((16, DK, BLK), BF16),
            pltpu.VMEM((KEYS, 2 * BLK), F32),
            pltpu.VMEM((KEYS, 2 * BLK), F32),
            pltpu.VMEM((KEYS, BLK), F32),
            pltpu.SemaphoreType.DMA,
        ],
        "attention_target",
    )(block_counts, stats, in_vmem(latent_t), in_hbm(q_t), in_vmem(q_other))
    arrived_targets = {s: lax.ppermute(targets[s], "y", ring(s)) for s in SHIFTS}

    grads = call(
        loss_kernel,
        shape((LG_ROWS, BLK), BF16),
        [VMEM] * 5,
        VMEM,
        name="loss",
    )(*map(in_vmem, (targets[0], *(arrived_targets[s] for s in (1, 2, 3)), logits)))
    x_own, _ = lax.optimization_barrier((x_own, grads))
    x_other = lax.ppermute(x_own, "c", SWAP)
    grads_all = around_y(grads)

    query_grad, entropy = call(
        backward_kernel,
        (shape((2 * NQ, COLS, BLK), BF16), shape((8, BLK), F32)),
        [VMEM] * 8,
        (VMEM, VMEM),
        [pltpu.VMEM((KEYS, BLK), F32)],
        "index_backward",
    )(*map(in_vmem, (*grads_all, index_keys, index_t, *iq_pair)))
    entropy_other = lax.ppermute(entropy, "c", SWAP)
    entropy_both = jnp.where(
        first,
        jnp.concatenate([entropy[0], entropy_other[0]]),
        jnp.concatenate([entropy_other[0], entropy[0]]),
    )
    share = 2 * BLK // (2 * NY)
    entropy_mine = lax.dynamic_slice_in_dim(entropy_both, (2 * y + core) * share, share, 0)

    swapped = lax.all_to_all(query_grad, ("z", "x", "c"), split_axis=0, concat_axis=0, tiled=True)
    qblk = ("z", "x")
    piece = call(
        weight_kernel,
        shape((COLS, DQ), BF16),
        [VMEM, ANY, VMEM],
        VMEM,
        [
            pltpu.VMEM((COLS, QUERIES), BF16),
            pltpu.VMEM((QUERIES, half), BF16),
            pltpu.SemaphoreType.DMA((4,)),
        ],
        "weight_piece",
    )(in_vmem(swapped), in_hbm(x_own), in_vmem(x_other))
    same = [piece] + [lax.ppermute(piece, qblk, plane(-2 * d, d)) for d in (1, 2, 3)]
    full, top, bottom = call(
        quarter_kernel,
        (shape((DQ, 256), BF16), shape((half, 256), BF16), shape((half, 256), BF16)),
        [VMEM] * 4,
        (VMEM,) * 3,
        [pltpu.VMEM((256, DQ), BF16)],
        "quarter",
    )(*map(in_vmem, same))
    below = lax.ppermute(full, qblk, plane(1, 0))
    above = lax.ppermute(full, qblk, plane(-1, 0))
    top = lax.ppermute(top, qblk, plane(0, -1))
    bottom = lax.ppermute(bottom, qblk, plane(0, 1))
    wide = [pltpu.VMEM((2, DQ, 256), F32), pltpu.SemaphoreType.DMA((2,))]
    started = call(
        functools.partial(finish_kernel, (0, 2)),
        pltpu.HBM((DQ, HALF_COLS), F32),
        [VMEM] * 3,
        HBM,
        wide,
        "finish_first",
    )(*map(in_vmem, (full, top, bottom)))
    weight_grad = call(
        finish_rest_kernel,
        pltpu.HBM((DQ, HALF_COLS), F32),
        [HBM, VMEM, VMEM],
        HBM,
        wide,
        "finish_rest",
        {0: 0},
    )(in_hbm(started), in_vmem(below), in_vmem(above))
    return weight_grad, entropy_mine


def solution(mesh):
    fine = Mesh(mesh.devices.reshape(NY, 2, 4, 4), ("y", "c", "z", "x"))
    head, qblk = ("y", "c"), ("z", "x")
    placed = (
        P(qblk, head, None),
        P(qblk, None, None),
        P(qblk, None),
        P(None, head),
        P(qblk, head),
        P(),
        P(),
    )
    return jax.shard_map(
        on_device,
        mesh=fine,
        in_specs=placed,
        out_specs=(P(None, head), P(qblk + head)),
        check_vma=False,
    )
```

```python
import functools

import jax
import jax.numpy as jnp
from jax import lax
from jax.experimental import pallas as pl
from jax.experimental.pallas import tpu as pltpu
from jax.sharding import Mesh, PartitionSpec as P

BF16 = jnp.bfloat16
F32 = jnp.float32
I32 = jnp.int32

H = 128
DK = 576
ID = 128
CAP = 3
BLK = 128
SEL = 16
KEYS = SEL * BLK
NY = 4
NQ = 16
SHARD = 32
LATC = DK // NY
IDXC = ID // NY
PIECE = LATC + IDXC
OWNK = KEYS // NY
HALF_COLS = 1024
IQ_ROWS = HALF_COLS + 32
LG_ROWS = OWNK + 16
DQ = 1536
COLS = HALF_COLS // NQ
QUERIES = 4096

score_scale = 192.0 ** (-0.5)
exp2_scale = score_scale * 1.4426950408889634
masked_value = -1e30
VMEM_LIMIT = 24 * 1024 * 1024

ANY = pl.BlockSpec(memory_space=pl.ANY)
VMEM = pl.BlockSpec(memory_space=pltpu.VMEM)
SMEM = pl.BlockSpec(memory_space=pltpu.SMEM)
HBM = pl.BlockSpec(memory_space=pltpu.HBM)


def call(kernel, out_shape, in_specs, out_specs, scratch=(), name=None, aliases=None):
    return pl.pallas_call(
        kernel,
        out_shape=out_shape,
        in_specs=in_specs,
        out_specs=out_specs,
        scratch_shapes=list(scratch),
        compiler_params=pltpu.CompilerParams(vmem_limit_bytes=VMEM_LIMIT),
        name=name,
        input_output_aliases=aliases or {},
    )


def shape(dims, dtype):
    return jax.ShapeDtypeStruct(dims, dtype)


def in_hbm(array):
    return pltpu.with_memory_space_constraint(array, pltpu.HBM)


def in_vmem(array):
    return pltpu.with_memory_space_constraint(array, pltpu.VMEM)


def place():
    return lax.axis_index("y"), lax.axis_index("c"), lax.axis_index(("z", "x"))


def slots_in_use(counts):
    _, core, me = place()
    return counts[2 * me + core]


def pick_outgoing_kernel(ids, cache, out, found, sem):
    y, core, me = place()
    rows = pl.ds(pl.multiple_of(y * PIECE, 16), PIECE)
    first = me * SHARD

    def copy(block, place_out):
        return pltpu.make_async_copy(cache.at[block, rows, :], out.at[place_out], sem)

    def per_dst(dst, total):
        count = jnp.int32(0)
        for s in range(SEL):
            local = ids[s, 2 * dst + core] - first
            found[total + count] = local * (NQ * CAP) + dst * CAP + jnp.minimum(count, CAP - 1)
            count = count + ((local >= 0) & (local < SHARD)).astype(I32)
        return total + count

    total = lax.fori_loop(0, NQ, per_dst, jnp.int32(0))

    def start(n, carry):
        code = found[n]
        block = code // (NQ * CAP)
        copy(block, code - block * (NQ * CAP)).start()
        return carry

    def wait(n, carry):
        copy(0, 0).wait()
        return carry

    lax.fori_loop(0, total, start, 0)
    lax.fori_loop(0, total, wait, 0)


def pick_listed_kernel(ids, arrived, *refs):
    low, high, listed, seen, sem = refs[-5:]
    _, core, me = place()
    row = 2 * me + core
    for i in range(NQ):
        seen[i] = 0
    pending = []
    for s in range(SEL):
        owner = lax.shift_right_logical(ids[s, row], 5)
        rank = jnp.minimum(seen[owner], CAP - 1)
        seen[owner] = seen[owner] + 1
        pending.append(pltpu.make_async_copy(arrived.at[owner * CAP + rank], listed.at[s], sem.at[0]))
        pending[-1].start()
    for c in pending:
        c.wait()
    half = SEL // 2
    outs = [
        pltpu.make_async_copy(listed.at[pl.ds(n * half, half)], out, sem.at[1])
        for n, out in enumerate((low, high))
    ]
    for c in outs:
        c.start()
    for c in outs:
        c.wait()


def index_query_kernel(x, w, hw, mine, other):
    core = lax.axis_index("c")
    for k in range(4):
        cols = HALF_COLS // 4
        part = jnp.dot(x[...], w[:, k * cols : (k + 1) * cols], preferred_element_type=F32)
        part = part.astype(BF16)
        low = part[:BLK].T
        high = part[BLK:].T
        rows = pl.ds(k * cols, cols)
        first = jnp.broadcast_to(core == 0, low.shape)
        mine[rows, :] = jnp.where(first, low, high)
        other[rows, :] = jnp.where(first, high, low)
    weights = hw[...]
    hi = weights.astype(BF16)
    rest = weights - hi.astype(F32)
    mid = rest.astype(BF16)
    lo = (rest - mid.astype(F32)).astype(BF16)
    ext = jnp.concatenate(
        [hi.astype(F32), mid.astype(F32), lo.astype(F32), jnp.zeros_like(weights)], axis=0
    )
    first = jnp.broadcast_to(core == 0, (32, BLK))
    tail = pl.ds(HALF_COLS, 32)
    mine[tail, :] = jnp.where(first, ext[:, :BLK], ext[:, BLK:]).astype(BF16)
    other[tail, :] = jnp.where(first, ext[:, BLK:], ext[:, :BLK]).astype(BF16)


def head_rows(tail):
    tail = tail.astype(F32)
    return tail[0:8] + tail[8:16] + tail[16:24]


def logits_kernel(counts, own_low, own_high, a1, b1, a2, b2, a3, b3, *refs):
    iq_refs, rest = refs[:8], refs[8:]
    logits_ref, stats_ref, latent_t, keys_out, keys_t_out, index_t, keys, total, own, sems = rest
    y, count = lax.axis_index("y"), slots_in_use(counts)
    half = SEL // 2
    loads = [
        pltpu.make_async_copy(own_low, own.at[pl.ds(0, half)], sems.at[2]),
        pltpu.make_async_copy(own_high, own.at[pl.ds(half, half)], sems.at[3]),
    ]
    for c in loads:
        c.start()
    for s, low, high in ((1, a1, b1), (2, a2, b2), (3, a3, b3), (0, own, own.at[pl.ds(half, half)])):
        if s == 0:
            for c in loads:
                c.wait()
        rows = pl.ds(pl.multiple_of(lax.rem(y + NY - s, NY) * PIECE, 16), PIECE)
        for j in range(half):
            keys[rows, j * BLK : (j + 1) * BLK] = low[j]
            keys[rows, (half + j) * BLK : (half + j + 1) * BLK] = high[j]
    copies = [pltpu.make_async_copy(keys.at[pl.ds(DK, ID), :], keys_out, sems.at[0])]
    copies[0].start()
    for j in range(SEL):
        span = slice(j * BLK, (j + 1) * BLK)
        latent_t[span, :] = keys[:DK, span].T
        index_t[span, :] = keys[DK:, span].T
    copies.append(pltpu.make_async_copy(index_t, keys_t_out, sems.at[1]))
    copies[1].start()
    keys_t = index_t[pl.ds(pl.multiple_of(y * OWNK, OWNK), OWNK), :]
    total[...] = jnp.zeros_like(total)
    for ref in iq_refs:
        rows = head_rows(ref[HALF_COLS:, :])
        for p in range(4):
            a, b = 2 * p, 2 * p + 1
            pair = jnp.concatenate(
                [ref[a * ID : (a + 1) * ID, :], ref[b * ID : (b + 1) * ID, :]], axis=1
            )
            affinity = jnp.maximum(jnp.dot(keys_t, pair, preferred_element_type=F32), 0.0)
            total[...] += (
                affinity[:, :BLK] * rows[a : a + 1] + affinity[:, BLK:] * rows[b : b + 1]
            )
    key = lax.broadcasted_iota(I32, (OWNK, BLK), 0) + y * OWNK
    token = lax.broadcasted_iota(I32, (OWNK, BLK), 1)
    valid = (key < count * BLK) & ((key >= BLK) | (key <= token))
    masked = jnp.where(valid, total[...], masked_value)
    logits_ref[...] = masked
    peak = jnp.max(masked, axis=0, keepdims=True)
    mass = jnp.sum(jnp.exp(masked - peak), axis=0, keepdims=True)
    row = lax.broadcasted_iota(I32, (8, BLK), 0)
    stats_ref[...] = jnp.where(row == 0, peak, mass)
    for c in copies:
        c.wait()


def split_rows(row):
    hi = row.astype(BF16).astype(F32)
    mid = (row - hi).astype(BF16).astype(F32)
    return hi, mid, row - hi - mid


def tail_tile(rows):
    at = lax.broadcasted_iota(I32, (16, BLK), 0)
    tile = jnp.zeros((16, BLK), F32)
    for n, row in enumerate(rows):
        tile = jnp.where(at == n, row, tile)
    return tile.astype(BF16)


def target_kernel(
    counts, stats, keys_t, q_own, qb, o0, o1, o2, o3, qa, buf_a, buf_b, total, sem
):
    y, core, _ = place()
    count = slots_in_use(counts)
    lanes = pl.multiple_of(core * BLK, BLK)
    early = 2
    spans = (pl.ds(0, early), pl.ds(early, qa.shape[0] - early))
    loads = [
        pltpu.make_async_copy(q_own.at[span, :, pl.ds(lanes, BLK)], qa.at[span], sem.at[n])
        for n, span in enumerate(spans)
    ]
    for c in loads:
        c.start()
    total[...] = jnp.zeros_like(total)
    loads[0].wait()

    chunk = 1024
    token = lax.broadcasted_iota(I32, (BLK, 2 * BLK), 1) % BLK
    causal = lax.broadcasted_iota(I32, (BLK, 2 * BLK), 0) <= token

    def rows_of(tile):
        return tile.reshape(tile.shape[0] // 8, 8, 2 * BLK)

    def score_part(pair, buf, k, peak):
        part = jnp.dot(keys_t[k * chunk : (k + 1) * chunk, :], pair, preferred_element_type=F32)
        for j in range(chunk // BLK):
            slot = k * (chunk // BLK) + j
            tile = part[j * BLK : (j + 1) * BLK]
            if slot == 0:
                tile = jnp.where(causal, tile, masked_value)
            buf[slot * BLK : (slot + 1) * BLK, :] = tile
            top = jnp.max(rows_of(tile), axis=0)
            peak = jnp.maximum(peak, jnp.where(slot < count, top, masked_value))
        return peak

    def exp_part(buf, k, shift, mass):
        span = slice(k * BLK, (k + 1) * BLK)
        tile = jnp.exp2(buf[span, :] * exp2_scale - shift)
        buf[span, :] = tile
        return mass + jnp.where(k < count, jnp.sum(rows_of(tile), axis=0), 0.0)

    def add_part(buf, k, share):
        span = slice(k * BLK, (k + 1) * BLK)
        tile = buf[span, :] * share
        total[span, :] += tile[:, :BLK] + tile[:, BLK:]

    low = jnp.full((8, 2 * BLK), masked_value, F32)
    parts = KEYS // chunk
    step_slots = SEL // (parts // 2)

    def both(p, buf, done, shift):
        peak = low
        if p is not None:
            pair = jnp.concatenate([qa[p], qb[p]], axis=1)
        mass = jnp.zeros((8, 2 * BLK), F32)
        for k in range(parts // 2):
            if p is not None:
                peak = score_part(pair, buf, k, peak)
            if done is not None:
                for n in range(step_slots * k, step_slots * (k + 1)):
                    mass = exp_part(done, n, shift, mass)
        if done is not None:
            share = 1.0 / (jnp.sum(mass, axis=0, keepdims=True) * H)
        for k in range(parts // 2):
            if p is not None:
                peak = score_part(pair, buf, parts // 2 + k, peak)
            if done is not None:
                for n in range(step_slots * k, step_slots * (k + 1)):
                    add_part(done, n, share)
        return jnp.max(peak, axis=0, keepdims=True) * exp2_scale

    def step(k, shift):
        shift = both(2 * k + 1, buf_b, buf_a, shift)
        return both(2 * k + 2, buf_a, buf_b, shift)

    pairs = qa.shape[0]
    shift = both(0, buf_a, None, None)
    loads[1].wait()
    shift = lax.fori_loop(0, pairs // 2 - 1, step, shift)
    shift = both(pairs - 1, buf_b, buf_a, shift)
    both(None, None, buf_b, shift)
    tail = tail_tile(split_rows(stats[0:1, :]) + split_rows(stats[1:2, :]))
    for s, out in enumerate((o0, o1, o2, o3)):
        start = pl.multiple_of(lax.rem(y + s, NY) * OWNK, OWNK)
        used = lax.broadcasted_iota(I32, (OWNK, BLK), 0) + start < count * BLK
        out[:OWNK, :] = jnp.where(used, total[pl.ds(start, OWNK), :], 0.0).astype(BF16)
        out[OWNK:, :] = tail


def loss_kernel(t0, t1, t2, t3, logits, out):
    pieces = (t0, t1, t2, t3)
    tails = [t[OWNK:, :].astype(F32) for t in pieces]
    peaks = [t[0:1] + t[1:2] + t[2:3] for t in tails]
    masses = [t[3:4] + t[4:5] + t[5:6] for t in tails]
    peak = functools.reduce(jnp.maximum, peaks)
    mass = functools.reduce(jnp.add, [m * jnp.exp(p - peak) for m, p in zip(masses, peaks)])
    log_total = peak + jnp.log(mass)
    target = functools.reduce(jnp.add, [t[:OWNK, :].astype(F32) for t in pieces])
    masked = logits[...]
    valid = masked > 0.5 * masked_value
    log_probs = masked - log_total
    entropy = -jnp.sum(jnp.where(valid, target * log_probs, 0.0), axis=0, keepdims=True)
    grad = jnp.where(valid, jnp.exp(log_probs) - target, 0.0) / QUERIES
    out[:OWNK, :] = grad.astype(BF16)
    out[OWNK:, :] = tail_tile(split_rows(entropy))


def backward_kernel(g0, g1, g2, g3, keys, keys_t, iq_first, iq_second, out, entropy_ref, grads):
    y = lax.axis_index("y")
    entropy = jnp.zeros((1, BLK), F32)
    for s, piece in enumerate((g0, g1, g2, g3)):
        start = pl.multiple_of(lax.rem(y + NY - s, NY) * OWNK, OWNK)
        grads[pl.ds(start, OWNK), :] = piece[:OWNK, :].astype(F32)
        tail = piece[OWNK:, :].astype(F32)
        entropy = entropy + tail[0:1] + tail[1:2] + tail[2:3]
    entropy_ref[...] = jnp.broadcast_to(entropy, (8, BLK))
    chunk = 512
    for core, ref in enumerate((iq_first, iq_second)):
        rows = head_rows(ref[HALF_COLS:, :])
        for p in range(4):
            a, b = 2 * p, 2 * p + 1
            pair = jnp.concatenate(
                [ref[a * ID : (a + 1) * ID, :], ref[b * ID : (b + 1) * ID, :]], axis=1
            )
            acc = jnp.zeros((ID, 2 * BLK), F32)
            for k in range(KEYS // chunk):
                span = slice(k * chunk, (k + 1) * chunk)
                affinity = jnp.dot(keys_t[span, :], pair, preferred_element_type=F32)
                grad = grads[span, :]
                scaled = jnp.concatenate([grad * rows[a : a + 1], grad * rows[b : b + 1]], axis=1)
                masked = jnp.where(affinity > 0, scaled, 0.0).astype(BF16)
                acc = acc + jnp.dot(keys[:, span], masked, preferred_element_type=F32)
            acc = acc.astype(BF16)
            for n, head in enumerate((a, b)):
                lanes = slice(n * BLK, (n + 1) * BLK)
                out[2 * owner_of_piece(2 * head) + core] = acc[:COLS, lanes]
                out[2 * owner_of_piece(2 * head + 1) + core] = acc[COLS:, lanes]


def owner_of_piece(piece):
    k, x = piece // 4, piece % 4
    return (k - 2 * x) % 4 * 4 + x


def weight_kernel(qg, xa, xb, out, lhs, own_x, sems):
    parts = sems.shape[0]
    span = QUERIES // parts
    copies = []
    for k in range(parts):
        rows = pl.ds(k * span, span)
        copies.append(pltpu.make_async_copy(xa.at[rows, :], own_x.at[rows, :], sems.at[k]))
        copies[-1].start()
    for s in range(2 * NQ):
        lhs[:, s * BLK : (s + 1) * BLK] = qg[s]
    other = jnp.dot(lhs[...], xb[...], preferred_element_type=F32).astype(BF16)
    own = jnp.zeros(other.shape, F32)
    for k in range(parts):
        rows = slice(k * span, (k + 1) * span)
        copies[k].wait()
        own = own + jnp.dot(lhs[:, rows], own_x[rows, :], preferred_element_type=F32)
    own = own.astype(BF16)
    own_first = jnp.broadcast_to(lax.axis_index("c") == 0, own.shape)
    half = own.shape[1]
    out[:, :half] = jnp.where(own_first, own, other)
    out[:, half:] = jnp.where(own_first, other, own)


def quarter_kernel(p0, p1, p2, p3, full, top, bottom, rows):
    x = lax.axis_index("x")
    for s, piece in enumerate((p0, p1, p2, p3)):
        start = pl.multiple_of(lax.rem(x + 4 - s, 4) * COLS, COLS)
        rows[pl.ds(start, COLS), :] = piece[...]
    for k in range(6):
        tile = rows[:, k * 256 : (k + 1) * 256].T
        full[k * 256 : (k + 1) * 256, :] = tile
        half = top if k < 3 else bottom
        half[k % 3 * 256 : (k % 3 + 1) * 256, :] = tile


def finish_kernel(shifts, *refs):
    pieces, (out, wide, sems) = refs[:-3], refs[-3:]
    colour = lax.rem(lax.axis_index("z") + 2 * lax.axis_index("x"), 4)
    copies, at = [], 0
    for n, shift in enumerate(shifts):
        row = 0
        while row < DQ:
            piece = pieces[at]
            wide[n, row : row + piece.shape[0], :] = piece[...].astype(F32)
            row, at = row + piece.shape[0], at + 1
        lanes = pl.multiple_of(lax.rem(colour + shift, 4) * 256, 256)
        copies.append(pltpu.make_async_copy(wide.at[n], out.at[:, pl.ds(lanes, 256)], sems.at[n]))
        copies[-1].start()
    for c in copies:
        c.wait()


def finish_rest_kernel(started, *refs):
    del started
    finish_kernel((3, 1), *refs)


def plane(dz, dx):
    return [
        (z * 4 + x, (z + dz) % 4 * 4 + (x + dx) % 4) for z in range(4) for x in range(4)
    ]


def ring(shift):
    return [(i, (i + shift) % NY) for i in range(NY)]


SWAP = [(0, 1), (1, 0)]
SHIFTS = (1, 3, 2)


def relayed(low, high):
    low_up, high_down = lax.ppermute(low, "y", ring(1)), lax.ppermute(high, "y", ring(3))
    high_up, low_down = lax.ppermute(high, "y", ring(1)), lax.ppermute(low, "y", ring(3))
    low_far, high_far = lax.ppermute(low_up, "y", ring(1)), lax.ppermute(high_down, "y", ring(3))
    return low_up, high_up, low_far, high_far, low_down, high_down


def around_y(array):
    moved = {s: lax.ppermute(array, "y", ring(s)) for s in SHIFTS}
    return (array, moved[1], moved[2], moved[3])


def on_device(
    q_absorbed, key_cache, index_input, index_weight, head_weights, block_ids, block_counts
):
    y, core, _ = place()
    ids = block_ids.T

    outgoing = call(
        pick_outgoing_kernel,
        shape((NQ * CAP, PIECE, BLK), BF16),
        [SMEM, ANY],
        VMEM,
        [pltpu.SMEM((NQ * SEL + 1,), I32), pltpu.SemaphoreType.DMA],
        "pick_outgoing",
    )(ids, in_hbm(key_cache))
    arrived = lax.all_to_all(outgoing, ("z", "x"), split_axis=0, concat_axis=0, tiled=True)

    iq_own, iq_send = call(
        index_query_kernel,
        (shape((IQ_ROWS, BLK), BF16),) * 2,
        [VMEM, VMEM, VMEM],
        (VMEM, VMEM),
        name="index_query",
    )(index_input, index_weight, head_weights.T)
    iq_other = lax.ppermute(iq_send, "c", SWAP)
    first = core == 0
    iq_pair = (jnp.where(first, iq_own, iq_other), jnp.where(first, iq_other, iq_own))
    iq_moved = relayed(*iq_pair)

    q_t = jnp.transpose(q_absorbed, (1, 2, 0))
    q_send = lax.dynamic_slice_in_dim(q_t, (1 - core) * BLK, BLK, 2)
    q_other = lax.ppermute(q_send, "c", SWAP)

    low, high = call(
        pick_listed_kernel,
        (pltpu.HBM((SEL // 2, PIECE, BLK), BF16),) * 2,
        [SMEM] + [ANY] * 8,
        (HBM, HBM),
        [
            pltpu.VMEM((SEL, PIECE, BLK), BF16),
            pltpu.SMEM((NQ,), I32),
            pltpu.SemaphoreType.DMA((2,)),
        ],
        "pick_listed",
    )(ids, arrived, q_send, *iq_moved)
    moved = relayed(low, high)

    half = DQ // 2
    x_half = lax.dynamic_slice_in_dim(index_input, core * half, half, 1)
    x_half, _ = lax.optimization_barrier((x_half, low))
    x_own = lax.all_gather(x_half, ("z", "x"), axis=0, tiled=True)

    logits, stats, latent_t, index_keys, index_t = call(
        logits_kernel,
        (
            shape((OWNK, BLK), F32),
            shape((8, BLK), F32),
            shape((KEYS, DK), BF16),
            pltpu.HBM((ID, KEYS), BF16),
            pltpu.HBM((KEYS, ID), BF16),
        ),
        [SMEM, ANY, ANY] + [VMEM] * 14,
        (VMEM, VMEM, VMEM, HBM, HBM),
        [
            pltpu.VMEM((KEYS, ID), BF16),
            pltpu.VMEM((DK + ID, KEYS), BF16),
            pltpu.VMEM((OWNK, BLK), F32),
            pltpu.VMEM((SEL, PIECE, BLK), BF16),
            pltpu.SemaphoreType.DMA((4,)),
        ],
        "index_logits",
    )(block_counts, in_hbm(low), in_hbm(high), *map(in_vmem, (*moved, *iq_pair, *iq_moved)))

    targets = call(
        target_kernel,
        (shape((LG_ROWS, BLK), BF16),) * 4,
        [SMEM, VMEM, VMEM, ANY, VMEM],
        (VMEM,) * 4,
        [
            pltpu.VMEM((16, DK, BLK), BF16),
            pltpu.VMEM((KEYS, 2 * BLK), F32),
            pltpu.VMEM((KEYS, 2 * BLK), F32),
            pltpu.VMEM((KEYS, BLK), F32),
            pltpu.SemaphoreType.DMA((2,)),
        ],
        "attention_target",
    )(block_counts, stats, in_vmem(latent_t), in_hbm(q_t), in_vmem(q_other))
    arrived_targets = {s: lax.ppermute(targets[s], "y", ring(s)) for s in SHIFTS}

    grads = call(
        loss_kernel,
        shape((LG_ROWS, BLK), BF16),
        [VMEM] * 5,
        VMEM,
        name="loss",
    )(*map(in_vmem, (targets[0], *(arrived_targets[s] for s in (1, 2, 3)), logits)))
    x_own, _ = lax.optimization_barrier((x_own, grads))
    x_other = lax.ppermute(x_own, "c", SWAP)
    grads_all = around_y(grads)

    query_grad, entropy = call(
        backward_kernel,
        (shape((2 * NQ, COLS, BLK), BF16), shape((8, BLK), F32)),
        [VMEM] * 8,
        (VMEM, VMEM),
        [pltpu.VMEM((KEYS, BLK), F32)],
        "index_backward",
    )(*map(in_vmem, (*grads_all, index_keys, index_t, *iq_pair)))
    entropy_other = lax.ppermute(entropy, "c", SWAP)
    entropy_both = jnp.where(
        first,
        jnp.concatenate([entropy[0], entropy_other[0]]),
        jnp.concatenate([entropy_other[0], entropy[0]]),
    )
    share = 2 * BLK // (2 * NY)
    entropy_mine = lax.dynamic_slice_in_dim(entropy_both, (2 * y + core) * share, share, 0)

    swapped = lax.all_to_all(query_grad, ("z", "x", "c"), split_axis=0, concat_axis=0, tiled=True)
    qblk = ("z", "x")
    piece = call(
        weight_kernel,
        shape((COLS, DQ), BF16),
        [VMEM, ANY, VMEM],
        VMEM,
        [
            pltpu.VMEM((COLS, QUERIES), BF16),
            pltpu.VMEM((QUERIES, half), BF16),
            pltpu.SemaphoreType.DMA((4,)),
        ],
        "weight_piece",
    )(in_vmem(swapped), in_hbm(x_own), in_vmem(x_other))
    same = [piece] + [lax.ppermute(piece, qblk, plane(-2 * d, d)) for d in (1, 2, 3)]
    full, top, bottom = call(
        quarter_kernel,
        (shape((DQ, 256), BF16), shape((half, 256), BF16), shape((half, 256), BF16)),
        [VMEM] * 4,
        (VMEM,) * 3,
        [pltpu.VMEM((256, DQ), BF16)],
        "quarter",
    )(*map(in_vmem, same))
    below = lax.ppermute(full, qblk, plane(1, 0))
    above = lax.ppermute(full, qblk, plane(-1, 0))
    top = lax.ppermute(top, qblk, plane(0, -1))
    bottom = lax.ppermute(bottom, qblk, plane(0, 1))
    wide = [pltpu.VMEM((2, DQ, 256), F32), pltpu.SemaphoreType.DMA((2,))]
    started = call(
        functools.partial(finish_kernel, (0, 2)),
        pltpu.HBM((DQ, HALF_COLS), F32),
        [VMEM] * 3,
        HBM,
        wide,
        "finish_first",
    )(*map(in_vmem, (full, top, bottom)))
    weight_grad = call(
        finish_rest_kernel,
        pltpu.HBM((DQ, HALF_COLS), F32),
        [HBM, VMEM, VMEM],
        HBM,
        wide,
        "finish_rest",
        {0: 0},
    )(in_hbm(started), in_vmem(below), in_vmem(above))
    return weight_grad, entropy_mine


def solution(mesh):
    fine = Mesh(mesh.devices.reshape(NY, 2, 4, 4), ("y", "c", "z", "x"))
    head, qblk = ("y", "c"), ("z", "x")
    placed = (
        P(qblk, head, None),
        P(qblk, None, None),
        P(qblk, None),
        P(None, head),
        P(qblk, head),
        P(),
        P(),
    )
    return jax.shard_map(
        on_device,
        mesh=fine,
        in_specs=placed,
        out_specs=(P(None, head), P(qblk + head)),
        check_vma=False,
    )
```
